128 devices in a mesh: req: 8 (over y_lo, x), exp: 16 (over z, y_hi, core).
Axes of the slice: x: 4, y: 4 (y_hi: 2, y_lo: 2; y = y_hi * 2 + y_lo), z: 4, core: 2. Of those that a mesh axis runs over, the one named last changes fastest.
Arguments:
- hidden_in: bfloat16 [2048, 6144], P(('req', 'exp')), may hold values from -6 to 6
- queries: bfloat16 [2048, 6144], P('req', 'exp'), may hold values from -25 to 25
- question_kv: bfloat16 [2048, 2048], P('req'), may hold values from -6 to 6
- passage_kv: bfloat16 [32, 2048, 2048], P('req', 'exp'), may hold values from -25 to 25
- use_lists: int32 [8, 4], replicated, may hold values from 0 to 31, as said below
- offsets: int32 [8, 4], replicated, may hold values from 0 to 6399, as said below
- out_weight: bfloat16 [6144, 6144], P('exp', 'req'), may hold values from -0.078125 to 0.078125
- norm_gain: float32 [6144], replicated, may hold values from 0.1 to 1.9
- router: bfloat16 [6144, 8], replicated, may hold values from -0.078125 to 0.078125
- routes: int32 [2048, 2], P(('req', 'exp')), may hold values from 0 to 7, all different within a row; in each aligned block of 16 rows (0 to 15, 16 to 31, ...) at most 5 rows name the same one
- w_gate: bfloat16 [8, 6144, 8192], P('req', None, 'exp'), may hold values from -0.078125 to 0.078125
- w_up: bfloat16 [8, 6144, 8192], P('req', None, 'exp'), may hold values from -0.078125 to 0.078125
- w_down: bfloat16 [8, 8192, 6144], P('req', 'exp'), may hold values from -0.0625 to 0.0625
Outputs:
- layer_out: bfloat16 [2048, 6144], P(('req', 'exp'))
The draws below stay inside these ranges and needn't reach their ends.
Inputs may be any that keep to these rules, and one draw needn't show every extreme that they name: `use_lists`: passage p lies with owner p // 4; the 4 passages of one request lie with 4 different owners. `offsets`: slot j starts at j * (2112) plus 0 to 63 positions. `routes`: in the rows of one device no expert is named more than 5 times; the two experts of a row differ.
All inputs are finite; a program needn't handle non-finite values.
Results may differ from the reference program's by a relative error of at most 0.014.
Values may be sent and summed in bfloat16 or wider, within the bound.
A program may use at most 128 MiB of HBM per device.

```python
import math
import jax
import jax.numpy as jnp
import numpy as np
from jax import lax

D = 6144
HQ = 48
KVH = 8
HD = 128
E = 8
H = 8192
PLEN = 2048
PUSE = 4
PASS_DEV = 4
GAP = 64
TOK_DEV = 16
C = 5
QTOK = 256
TOKENS = 2048
NPASS = 32
N_REQ = 8
N_EXP = 16


def draw_queries(key, part):
    key = jax.random.fold_in(key, 3)
    shape_all = (TOKENS, HQ * HD)
    base_key = jax.random.fold_in(key, 0)
    values = jax.random.truncated_normal(base_key, -6.0, 6.0, shape_all, jnp.float32)
    return values.astype(jnp.bfloat16)


def draw_passage_kv(key, part):
    key = jax.random.fold_in(key, 11)
    shape_all = (NPASS, PLEN, 2 * KVH * HD)
    values = jax.random.truncated_normal(key, -6.0, 6.0, shape_all, jnp.float32)
    return values.astype(jnp.bfloat16)


def draw_use_lists(key, part):
    key = jax.random.fold_in(key, 5)
    owner_key, local_key = jax.random.split(key)
    owner_keys = jax.random.split(owner_key, N_REQ)
    owners = jax.vmap(lambda single: jax.random.permutation(single, N_REQ)[:PUSE])(owner_keys)
    local_ids = jax.random.randint(local_key, (N_REQ, PUSE), 0, PASS_DEV)
    return (owners * PASS_DEV + local_ids).astype(jnp.int32)


def draw_offsets(key, part):
    key = jax.random.fold_in(key, 7)
    slot_ids = jnp.arange(PUSE, dtype=jnp.int32)[None, :]
    spare = jax.random.randint(key, (N_REQ, PUSE), 0, GAP)
    return (slot_ids * (PLEN + GAP) + spare).astype(jnp.int32)


def block_scale(rng, shape, cuts, smallest, largest):
    def one(axis_at, blocks):
        steps = jax.random.uniform(jax.random.fold_in(jax.random.fold_in(rng, 6), axis_at), (blocks,), jnp.float32, smallest / len(cuts), largest / len(cuts))
        return jnp.repeat(jnp.exp(steps), shape[axis_at] // blocks).reshape((-1,) + (1,) * (len(shape) - axis_at - 1))

    level = one(*cuts[0])
    for cut in cuts[1:]:
        level = level * one(*cut)
    return level


def deal_out(key, own, number, rows, number_of, top, limit, lean):
    sequence = jax.random.permutation(key, number_of)
    crowded, ordinary = shares(number_of, rows * top, limit, lean, True), shares(number_of, rows * top, limit, lean, False)
    places = jnp.arange(number_of)

    def named(sizes, offset_by):
        used = int((sizes > 0).sum())
        fixed = max(1, used // 4)
        moved = fixed + (places - fixed + offset_by * (used - fixed)) % max(1, number_of - fixed)
        return jnp.zeros((number_of,), jnp.int32).at[sequence[jnp.where(places < fixed, places, moved)]].set(jnp.asarray(sizes, jnp.int32))

    sizes = jnp.where(number % 4 == 0, named(crowded, number // 4), named(ordinary, number - number // 4 - 1))
    mixed = jax.random.permutation(jax.random.fold_in(own, 3), number_of)
    source_of, sink = mixed[0:number_of // 2 * 2:2], mixed[1:number_of // 2 * 2:2]
    slack = jnp.minimum(sizes[source_of] - 1, limit - sizes[sink]) // 2
    slack = jnp.where((source_of == sequence[0]) | (sink == sequence[0]) | (sizes[sink] == 0), 0, jnp.maximum(slack, 0))
    moved = jax.random.randint(jax.random.fold_in(own, 4), (number_of // 2,), 0, 1 << 20) % (slack + 1)
    sizes = sizes.at[source_of].add(-moved).at[sink].add(moved)
    items = jnp.searchsorted(jnp.cumsum(sizes), jnp.arange(rows * top), side="right").astype(jnp.int32)
    table = items.reshape(top, rows).T
    table = table[jax.random.permutation(jax.random.fold_in(own, 1), rows)]
    offset_by = jax.random.randint(jax.random.fold_in(own, 2), (rows, 1), 0, top)
    return jnp.take_along_axis(table, (jnp.arange(top)[None, :] + offset_by) % top, axis=1)


def shares(count, total, bound, slope, full):
    portions = [(1 << 20) // math.isqrt(grade ** slope) + 1 for grade in range(1, count + 1)]
    largest = bound if full else min(bound, max(-(-total // count), total * portions[0] // sum(portions)))
    least = 1 if total - largest >= count - 1 else 0
    counts, surplus = [largest] + [least] * (count - 1), total - largest - least * (count - 1)
    while surplus > 0:
        movable = [i for i in range(1, count) if counts[i] < largest] or [i for i in range(1, count) if counts[i] < bound]
        pool, remaining = sum([portions[i] for i in movable]), surplus
        for i in movable:
            addition = min(bound - counts[i], max(1, remaining * portions[i] // pool), surplus)
            counts[i] = counts[i] + addition
            surplus = surplus - addition
    return np.array(counts)


def noise(key, dims, spread, most, cuts=(), kind=jnp.bfloat16):
    drawn = jax.random.normal(key, dims, jnp.float32) * spread
    if len(cuts) > 0:
        drawn = block_scale(key, dims, cuts, -0.22, 0.18) * drawn
    return jnp.clip(drawn, min=-most, max=most).astype(kind)


def setup_inputs(seed: int = 0) -> dict:
    seeds = jax.random.split(jax.random.key(seed), 14)
    hidden_in = noise(seeds[0], (TOKENS, D), 1.0, 6.0, ((0, 128),))
    queries = draw_queries(jax.random.fold_in(seeds[13], 71), 0)
    question_kv = noise(seeds[2], (TOKENS, 2 * KVH * HD), 1.0, 6.0, ((0, 8),))
    passage_kv = draw_passage_kv(jax.random.fold_in(seeds[13], 71), 0)
    use_lists = draw_use_lists(jax.random.fold_in(seeds[13], 71), 0)
    offsets = draw_offsets(jax.random.fold_in(seeds[13], 71), 0)
    out_weight = noise(seeds[6], (HQ * HD, D), (HQ * HD) ** -0.5, 0.078125, ((0, 16), (1, 8)))
    norm_gain = jnp.clip(1.0 + 0.18 * jax.random.normal(seeds[7], (D,), jnp.float32), 0.1, 1.9)
    router = noise(seeds[8], (D, E), D ** -0.5, 0.078125)
    routes_keys = jax.random.split(jax.random.fold_in(seeds[9], 1), TOKENS // TOK_DEV)
    routes_turns = jax.random.permutation(jax.random.fold_in(seeds[9], 3), TOKENS // TOK_DEV)
    routes = jax.vmap(lambda own, number: deal_out(jax.random.fold_in(seeds[9], 2), own, number, TOK_DEV, E, 2, C, 2))(routes_keys, routes_turns).reshape((TOKENS, 2))
    w_gate = noise(seeds[10], (E, D, H), D ** -0.5, 0.078125, ((0, 8), (2, 16)))
    w_up = noise(seeds[11], (E, D, H), D ** -0.5, 0.078125, ((0, 8), (2, 16)))
    w_down = noise(seeds[12], (E, H, D), H ** -0.5, 0.0625, ((0, 8), (1, 16)))
    return dict(hidden_in=hidden_in, queries=queries, question_kv=question_kv, passage_kv=passage_kv, use_lists=use_lists, offsets=offsets, out_weight=out_weight, norm_gain=norm_gain, router=router, routes=routes, w_gate=w_gate, w_up=w_up, w_down=w_down)


ROPE_BASE = 1000000.0
EPSILON = 1e-05

def frequencies():
    half_width = HD // 2
    return ROPE_BASE ** (-(jnp.arange(half_width, dtype=jnp.float32) / half_width))

def rotate(vectors, angles):
    half_width = HD // 2
    cosine = jnp.cos(angles)
    sine_part = jnp.sin(angles)
    lower = vectors[..., :half_width]
    upper = vectors[..., half_width:]
    return jnp.concatenate([lower * cosine - upper * sine_part, upper * cosine + lower * sine_part], axis=-1)

def head_attention(operands, allowed):
    grouped_q, head_keys, head_values = operands
    scores = jnp.einsum('gqd,kd->gqk', grouped_q.astype(jnp.float32), head_keys.astype(jnp.float32)) / math.sqrt(HD)
    scores = jnp.where(allowed[None], scores, -jnp.inf)
    highest = lax.optimization_barrier(jnp.max(scores, axis=-1, keepdims=True))
    weights = jnp.exp(scores - highest)
    probabilities = (weights / lax.optimization_barrier(jnp.sum(weights, axis=-1, keepdims=True))).astype(jnp.bfloat16)
    probabilities = lax.optimization_barrier(probabilities)
    mixed = jnp.einsum('gqk,kd->gqd', probabilities.astype(jnp.float32), head_values.astype(jnp.float32))
    return mixed.astype(jnp.bfloat16)

def reference(hidden_in, queries, question_kv, passage_kv, use_lists, offsets, out_weight, norm_gain, router, routes, w_gate, w_up, w_down):
    group_size = HQ // KVH
    freq_table = frequencies()
    q_angles = (PUSE * (PLEN + GAP) + jnp.arange(QTOK)).astype(jnp.float32)[:, None] * freq_table[None, :]
    causal = jnp.arange(QTOK)[:, None] >= jnp.arange(QTOK)[None, :]
    allowed = jnp.concatenate([jnp.ones((QTOK, PUSE * PLEN), dtype=bool), causal], axis=1)
    residual_parts = []
    for request in range(N_REQ):
        lo_row = request * QTOK
        chosen_kv = passage_kv[use_lists[request]].reshape(PUSE, PLEN, KVH, 2, HD)
        p_angles = offsets[request].astype(jnp.float32)[:, None, None, None] * freq_table
        p_keys = rotate(chosen_kv[:, :, :, 0, :].astype(jnp.float32), p_angles).astype(jnp.bfloat16)
        p_values = chosen_kv[:, :, :, 1, :]
        own_kv = question_kv[lo_row:lo_row + QTOK].reshape(QTOK, KVH, 2, HD)
        q_keys = rotate(own_kv[:, :, 0, :].astype(jnp.float32), q_angles[:, None, :]).astype(jnp.bfloat16)
        all_keys = jnp.concatenate([p_keys.reshape(PUSE * PLEN, KVH, HD), q_keys], axis=0)
        all_values = jnp.concatenate([p_values.reshape(PUSE * PLEN, KVH, HD), own_kv[:, :, 1, :]], axis=0)
        query_block = queries[lo_row:lo_row + QTOK].reshape(QTOK, HQ, HD).astype(jnp.float32)
        rotated = rotate(query_block, q_angles[:, None, :]).astype(jnp.bfloat16)
        grouped = rotated.reshape(QTOK, KVH, group_size, HD).transpose(1, 2, 0, 3)
        attended = lax.map(lambda operands: head_attention(operands, allowed), (grouped, all_keys.transpose(1, 0, 2), all_values.transpose(1, 0, 2)))
        attended = attended.transpose(2, 0, 1, 3).reshape(QTOK, HQ * HD)
        head_groups = attended.reshape(QTOK, N_EXP, HQ * HD // N_EXP).astype(jnp.float32)
        weight_groups = out_weight.reshape(N_EXP, HQ * HD // N_EXP, D).astype(jnp.float32)
        partials = jnp.einsum('tgc,gcd->gtd', head_groups, weight_groups).astype(jnp.bfloat16)
        partials = lax.optimization_barrier(partials).astype(jnp.float32)
        residual_parts.append(hidden_in[lo_row:lo_row + QTOK].astype(jnp.float32) + lax.optimization_barrier(jnp.sum(partials, axis=0)))
    resid = jnp.concatenate(residual_parts, axis=0)
    normed = (resid * lax.rsqrt(lax.optimization_barrier(jnp.mean(resid * resid, axis=-1, keepdims=True)) + EPSILON) * norm_gain).astype(jnp.bfloat16)
    logits = jnp.dot(normed, router, preferred_element_type=jnp.float32)
    expert_ids = jnp.arange(E, dtype=jnp.int32)
    selected = routes[:, :, None] == expert_ids[None, None, :]
    picked_logits = lax.optimization_barrier(jnp.sum(jnp.where(selected, logits[:, None, :], 0.0), axis=-1))
    gate_values = jax.nn.sigmoid(picked_logits - picked_logits[:, ::-1])
    block_count = TOKENS // TOK_DEV
    block_routes = routes.reshape(block_count, TOK_DEV * 2)
    one_hot = (block_routes[:, :, None] == expert_ids[None, None, :]).astype(jnp.int32)
    ranks = lax.optimization_barrier(jnp.sum((jnp.cumsum(one_hot, axis=1) - one_hot) * one_hot, axis=-1))
    slots = (jnp.arange(block_count, dtype=jnp.int32)[:, None] * C + ranks).reshape(-1).astype(jnp.int32)
    flat_routes = block_routes.reshape(-1).astype(jnp.int32)
    buffers = jnp.zeros((E, block_count * C, D), jnp.bfloat16).at[flat_routes, slots].set(jnp.repeat(normed, 2, axis=0))
    hidden_slice = H // N_EXP

    def expert_apply(operands):
        expert_rows, gate_part, up_part, down_part = operands
        inputs = expert_rows.astype(jnp.float32)
        gate_act = jnp.einsum('rd,djh->rjh', inputs, gate_part.astype(jnp.float32).reshape(D, N_EXP, hidden_slice))
        up_act = jnp.einsum('rd,djh->rjh', inputs, up_part.astype(jnp.float32).reshape(D, N_EXP, hidden_slice))
        inner = (jax.nn.silu(gate_act) * up_act).astype(jnp.bfloat16)
        inner = lax.optimization_barrier(inner).astype(jnp.float32)
        slice_out = jnp.einsum('rjh,jhd->rjd', inner, down_part.astype(jnp.float32).reshape(N_EXP, hidden_slice, D)).astype(jnp.bfloat16)
        slice_out = lax.optimization_barrier(slice_out).astype(jnp.float32)
        return lax.optimization_barrier(jnp.sum(slice_out, axis=1)).astype(jnp.bfloat16)
    expert_out = lax.map(expert_apply, (buffers, w_gate, w_up, w_down))
    fetched = expert_out[flat_routes, slots].reshape(TOKENS, 2, D).astype(jnp.float32)
    mixed = lax.optimization_barrier(jnp.sum(gate_values[:, :, None] * fetched, axis=1))
    return (resid + mixed).astype(jnp.bfloat16)
```

```python
import math

import jax
import jax.numpy as jnp
import numpy as np
from jax import lax
from jax.experimental import pallas as pl
from jax.experimental.pallas import tpu as pltpu
from jax.sharding import PartitionSpec as P

D = 6144
HALF = D // 2
HQ = 48
KVH = 8
HD = 128
E = 8
PLEN = 2048
PUSE = 4
PASS_DEV = 4
GAP = 64
C = 5
QTOK = 256
TOK = 16
N_REQ = 8
HID = 512
COLS = D // N_REQ
HEADS = 3
ROPE_BASE = 1000000.0
EPSILON = 1e-05
MESH = pl.DeviceIdType.MESH
F32 = jnp.float32
BF16 = jnp.bfloat16
VMEM = pl.BlockSpec(memory_space=pltpu.VMEM)
SMEM = pl.BlockSpec(memory_space=pltpu.SMEM)
ANY = pl.BlockSpec(memory_space=pl.ANY)
SCALE2 = math.log2(math.e) / math.sqrt(HD)
CHUNKS = (0, 1, 3, 2)


def place():
    req = lax.axis_index("req")
    exp = lax.axis_index("exp")
    return req, exp, exp // 4, (exp // 2) % 2, exp % 2


def member(z, yh, c):
    return (z * 2 + yh) * 2 + c


def remote(src, dst, send, recv, device):
    return pltpu.make_async_remote_copy(
        src_ref=src, dst_ref=dst, send_sem=send, recv_sem=recv, device_id=device, device_id_type=MESH
    )


def greet(devices):
    barrier = pltpu.get_barrier_semaphore()
    for device in devices:
        pl.semaphore_signal(barrier, inc=1, device_id=device, device_id_type=MESH)
    pl.semaphore_wait(barrier, len(devices))


def turn(vectors, cosine, sine):
    return vectors * cosine + pltpu.roll(vectors, HD // 2, vectors.ndim - 1) * sine


def attention_kernel(
    pkv, q_in, qkv, sel, own, pcos, psin, qcos, qsin, out,
    land0, land1, land2, land3, stage, got0, got1, got2, got3,
    kown, ksib, qrot, kvq, acc, top, low,
    s1s, s1r, s2s, s2r, fs, fr, ls,
):
    req, exp, z, yh, c = place()
    mine = req * 2 + yh
    land = (land0, land1, land2, land3)
    got = (got0, got1, got2, got3)
    sibling = (req, member(z, yh, 1 - c))
    head = exp // 2
    load_q = pltpu.make_async_copy(qkv.at[:, pl.ds(pl.multiple_of(head * 256, 256), 256)], kvq, ls)
    load_q.start()

    devices = [(req, member((z + d) % 4, yh, c)) for d in range(1, 4)] + [sibling]
    for k in range(1, 16):
        there = (mine + k) % 16
        devices.append((there // 2, member(z, there % 2, c)))
    greet(devices)

    def cols(zt):
        return pl.ds(pl.multiple_of(zt * 512, 512), 512)

    firsts = []
    for d in range(1, 4):
        zt = (z + d) % 4
        cp = remote(
            pkv.at[:, :, cols(zt)], land[4 - d], s1s.at[d], s1r.at[4 - d],
            (req, member(zt, yh, c)),
        )
        cp.start()
        firsts.append(cp)
    local = pltpu.make_async_copy(pkv.at[:, :, cols(z)], land0, s1r.at[0])
    local.start()

    def half(yt):
        return pl.ds(pl.multiple_of(yt * 256, 256), 256)

    def second(i, k):
        there = (mine + k) % 16
        return remote(
            stage.at[i, there // 2, :, half(there % 2)], got[i].at[mine],
            s2s.at[i, k], s2r.at[i, mine], (there // 2, member(z, there % 2, c)),
        )

    def second_in(i, k):
        there = (mine + k) % 16
        return remote(
            stage.at[i, there // 2, :, half(there % 2)], got[i].at[there],
            s2s.at[i, k], s2r.at[i, there], (there // 2, member(z, there % 2, c)),
        )

    def second_local(i):
        return pltpu.make_async_copy(
            stage.at[i, req, :, half(yh)], got[i].at[mine], s2r.at[i, mine]
        )

    def loop(count, body):
        lax.fori_loop(0, count, lambda k, carry: (body(k), carry)[1], 0)

    for i, d in enumerate(CHUNKS):
        if d == 0:
            local.wait()
        else:
            firsts[(4 - d) - 1].wait_recv()
        for r in range(N_REQ):
            stage[i, r] = land[d][sel[r]]
        loop(15, lambda k: second(i, k + 1).start())
        second_local(i).start()

        if i == 0:
            load_q.wait()
            cosine, sine = qcos[...], qsin[...]
            for h in range(HEADS):
                qrot[h] = turn(q_in[:, h * HD : (h + 1) * HD].astype(F32), cosine, sine).astype(BF16)
            keys = turn(kvq[:, :HD].astype(F32), cosine, sine).astype(BF16)
            values = kvq[:, HD:]
            row = lax.broadcasted_iota(jnp.int32, (QTOK, QTOK), 0)
            col = lax.broadcasted_iota(jnp.int32, (QTOK, QTOK), 1)
            for h in range(HEADS):
                s = lax.dot_general(
                    qrot[h], keys, (((1,), (1,)), ((), ())), preferred_element_type=F32
                )
                s = jnp.where(col <= row, s, -jnp.inf)
                t = jnp.max(s, axis=-1, keepdims=True)
                p = jnp.exp2(s * SCALE2 - t * SCALE2)
                top[h] = jnp.broadcast_to(t, (QTOK, HD))
                low[h] = jnp.broadcast_to(jnp.sum(p, axis=-1, keepdims=True), (QTOK, HD))
                acc[h] = jnp.dot(p.astype(BF16), values, preferred_element_type=F32)

    def attend(block):
        def one(h):
            s = lax.dot_general(
                qrot[h], block[:, :HD], (((1,), (1,)), ((), ())), preferred_element_type=F32
            )
            before = top[h][:, :1]
            t = jnp.maximum(before, jnp.max(s, axis=-1, keepdims=True))
            p = jnp.exp2(s * SCALE2 - t * SCALE2)
            alpha = jnp.exp2((before - t) * SCALE2)
            top[h] = jnp.broadcast_to(t, (QTOK, HD))
            low[h] = low[h] * alpha + jnp.sum(p, axis=-1, keepdims=True)
            acc[h] = acc[h] * alpha + jnp.dot(
                p.astype(BF16), block[:, HD:], preferred_element_type=F32
            )

        loop(HEADS, one)

    passes = []
    for i in range(4):
        loop(15, lambda k: second_in(i, k + 1).wait_recv())
        second_local(i).wait()
        for j in range(PUSE):
            cosine, sine = pcos[pl.ds(j, 1), :], psin[pl.ds(j, 1), :]
            for y in range(2):
                kv = got[i][own[j] * 2 + y]
                rows = pl.ds(j * 256 + y * 128, 128)
                kown[i, rows, :HD] = turn(kv[:, :HD].astype(F32), cosine, sine).astype(BF16)
                kown[i, rows, HD:] = kv[:, HD:]
        cp = remote(kown.at[i], ksib.at[i], fs.at[i], fr.at[i], sibling)
        cp.start()
        passes.append(cp)
        attend(kown.at[i])
        cp.wait_recv()
        attend(ksib.at[i])

    for h in range(HEADS):
        out[:, h * HD : (h + 1) * HD] = (acc[h] / low[h]).astype(BF16)
    for cp in firsts:
        cp.wait_send()
    for i in range(4):
        loop(15, lambda k: second(i, k + 1).wait_send())
        passes[i].wait_send()


def attention(passage_kv, queries, question_kv, sel, own, pcos, psin, qcos, qsin):
    dma = pltpu.SemaphoreType.DMA
    return pl.pallas_call(
        attention_kernel,
        out_shape=jax.ShapeDtypeStruct((QTOK, HEADS * HD), BF16),
        in_specs=[ANY, VMEM, ANY, SMEM, SMEM, VMEM, VMEM, VMEM, VMEM],
        out_specs=VMEM,
        scratch_shapes=[pltpu.VMEM((PASS_DEV, 128, 512), BF16)] * 4
        + [pltpu.VMEM((4, N_REQ, 128, 512), BF16)]
        + [pltpu.VMEM((16, 128, 256), BF16)] * 4
        + [
            pltpu.VMEM((4, 1024, 256), BF16),
            pltpu.VMEM((4, 1024, 256), BF16),
            pltpu.VMEM((HEADS, QTOK, HD), BF16),
            pltpu.VMEM((QTOK, 256), BF16),
            pltpu.VMEM((HEADS, QTOK, HD), F32),
            pltpu.VMEM((HEADS, QTOK, HD), F32),
            pltpu.VMEM((HEADS, QTOK, HD), F32),
            dma((4,)), dma((4,)), dma((4, 16)), dma((4, 16)), dma((4,)), dma((4,)), dma,
        ],
        name="attend_passages",
        compiler_params=pltpu.CompilerParams(
            collective_id=0, has_side_effects=True, vmem_limit_bytes=48 << 20
        ),
    )(passage_kv, queries, question_kv, sel, own, pcos, psin, qcos, qsin)


def project_kernel(
    att, w, hid, gain, router, spots, diff, first, second, resid_out, packed_out, gates_out,
    attb, ownp, sibs, sibr, rss, rsr, fsend, fin, nsend, nbuf, pbuf, gbuf,
    a_s, a_r, b_s, b_r, c_s, c_r, d_s, d_r, e_s, e_r,
):
    req, exp, z, yh, c = place()
    chip = exp // 2
    sibling = (req, member(z, yh, 1 - c))
    peers = [((req + d) % N_REQ, exp) for d in range(1, 8)]
    chips = [(req, ((chip + d) % 8) * 2 + c) for d in range(1, 8)]
    greet(peers + chips + [sibling])

    sends = []
    for d in range(7, 0, -1):
        cp = remote(att, attb.at[8 - d], a_s.at[d], a_r.at[8 - d], peers[d - 1])
        cp.start()
        sends.append(cp)
    by_turn = {8 - d: cp for d, cp in zip(range(7, 0, -1), sends)}

    def multiply(k):
        source = att if k == 0 else attb.at[k]
        if k > 0:
            by_turn[k].wait_recv()
        theirs = source[:, 1 - c].reshape(128, 384)
        sibs[k] = jnp.dot(theirs, w[...], preferred_element_type=F32).astype(BF16).reshape(8, TOK, COLS)
        cp = remote(sibs.at[k], sibr.at[k], b_s.at[k], b_r.at[k], sibling)
        cp.start()
        ours = source[:, c].reshape(128, 384)
        ownp[k] = jnp.dot(ours, w[...], preferred_element_type=F32).reshape(8, TOK, COLS)
        return cp

    def scatter(k, cp):
        cp.wait_recv()
        rss[k] = (ownp[k] + sibr[k].astype(F32)).astype(BF16)
        rsr[k, chip] = rss[k, chip]
        copies = []
        for d in range(1, 8):
            there = (chip + d) % 8
            cp = remote(rss.at[k, there], rsr.at[k, chip], c_s.at[k, d], c_r.at[k, d], chips[d - 1])
            cp.start()
            copies.append(cp)
        return copies

    def finish(k, copies):
        for cp in copies:
            cp.wait_recv()
        total = jnp.sum(rsr[k].astype(F32), axis=0).astype(BF16)
        if k == 0:
            fin[req] = total
            return None
        fsend[k] = total
        cp = remote(fsend.at[k], fin.at[req], d_s.at[k], d_r.at[k], peers[k - 1])
        cp.start()
        return cp

    halves, parts, ends = {}, {}, {}
    for k in range(8 + 4):
        if k < 8:
            halves[k] = multiply(k)
        if 0 <= k - 1 < 8:
            parts[k - 1] = scatter(k - 1, halves[k - 1])
        if 0 <= k - 4 < 8:
            ends[k - 4] = finish(k - 4, parts[k - 4])
    for k in range(1, 8):
        ends[k].wait_recv()

    attn = jnp.concatenate([fin[i] for i in range(N_REQ)], axis=1).astype(F32)
    resid = hid[...].astype(F32) + attn
    resid_out[...] = resid
    mean = jnp.mean(resid * resid, axis=-1, keepdims=True)
    normed = (resid * lax.rsqrt(mean + EPSILON) * gain[...]).astype(BF16)

    left, right = normed[:, :HALF], normed[:, HALF:]
    nsend[...] = jnp.where(c == 0, right, left)
    nbuf[c] = jnp.where(c == 0, left, right)
    pbuf[c] = spots[...]
    lasts = [
        remote(nsend, nbuf.at[c], e_s.at[0], e_r.at[0], sibling),
        remote(spots, pbuf.at[c], e_s.at[1], e_r.at[1], sibling),
    ]
    for cp in lasts:
        cp.start()
    logits = jnp.dot(normed, router[...], preferred_element_type=F32)
    apart = jnp.sum(logits * diff[...], axis=-1, keepdims=True)
    gates = first[...] * jax.nn.sigmoid(apart) + second[...] * jax.nn.sigmoid(-apart)
    gbuf[c] = gates
    cp = remote(gbuf.at[c], gbuf.at[c], e_s.at[2], e_r.at[2], sibling)
    cp.start()
    lasts.append(cp)
    lasts[0].wait_recv()
    lasts[1].wait_recv()
    packed_out[...] = (
        lax.dot_general(
            pbuf[...].reshape(32, 128), nbuf[...].reshape(32, HALF), (((0,), (0,)), ((), ())),
            preferred_element_type=F32,
        )
        .astype(BF16)
        .reshape(E, TOK, HALF)
    )
    lasts[2].wait_recv()
    gates_out[...] = gbuf[...]

    for cp in sends + lasts:
        cp.wait_send()
    for k in range(8):
        halves[k].wait_send()
        for cp in parts[k]:
            cp.wait_send()
        if k > 0:
            ends[k].wait_send()


def project(att, w, hid, gain, router, spots, diff, first, second):
    dma = pltpu.SemaphoreType.DMA
    v = pltpu.VMEM
    return pl.pallas_call(
        project_kernel,
        out_shape=(
            jax.ShapeDtypeStruct((TOK, D), F32),
            jax.ShapeDtypeStruct((E, TOK, HALF), BF16),
            jax.ShapeDtypeStruct((2, TOK, 128), F32),
        ),
        in_specs=[VMEM] * 9,
        out_specs=(VMEM,) * 3,
        scratch_shapes=[
            v((8, 8, 2, TOK, 384), BF16),
            v((8, 8, TOK, COLS), F32),
            v((8, 8, TOK, COLS), BF16),
            v((8, 8, TOK, COLS), BF16),
            v((8, 8, TOK, COLS), BF16),
            v((8, 8, TOK, COLS), BF16),
            v((8, TOK, COLS), BF16),
            v((8, TOK, COLS), BF16),
            v((TOK, HALF), BF16),
            v((2, TOK, HALF), BF16),
            v((2, TOK, 128), BF16),
            v((2, TOK, 128), F32),
            dma((8,)), dma((8,)), dma((8,)), dma((8,)), dma((8, 8)), dma((8, 8)),
            dma((8,)), dma((8,)), dma((3,)), dma((3,)),
        ],
        name="project_heads",
        compiler_params=pltpu.CompilerParams(
            collective_id=1, has_side_effects=True, vmem_limit_bytes=48 << 20
        ),
    )(att, w, hid, gain, router, spots, diff, first, second)


def expert_kernel(
    packed, gates, resid, pick, spread, wg_h, wu_h, wd_h, out,
    wg, wu, wd, prx, xo, xs, inner, po, sps, spr, rzs, rz, ysend, ry, bsend, ret, msend, mrecv,
    w_s, a_s, a_r, y_s, y_r, g_s, g_r, f_s, f_r, p_s, p_r, r_s, r_r, t_s, t_r, m_s, m_r,
):
    req, exp, z, yh, c = place()
    other = 1 - yh
    sibling = (req, member(z, yh, 1 - c))
    across = (req, member(z, other, c))
    up = (req, member((z + 1) % 4, yh, c))
    down = (req, member((z + 3) % 4, yh, c))
    peers = [((req + d) % N_REQ, exp) for d in range(1, 8)]
    loads = [
        pltpu.make_async_copy(src, dst, w_s.at[i])
        for i, (src, dst) in enumerate(((wg_h, wg), (wu_h, wu), (wd_h, wd)))
    ]
    for cp in loads:
        cp.start()
    greet(peers + [sibling, across, up, down])

    started = []

    def go(cp):
        cp.start()
        started.append(cp)
        return cp

    arrive = []
    for d in range(1, 8):
        there = (req + d) % N_REQ
        arrive.append(
            go(remote(packed.at[there], prx.at[req], a_s.at[d], a_r.at[d], peers[d - 1]))
        )
    prx[req] = packed[req]
    for cp in arrive:
        cp.wait_recv()
    xo[0, yh] = jnp.dot(
        pick[...], prx[...].reshape(128, HALF), preferred_element_type=F32
    ).astype(BF16)

    def share(i, zr, y):
        return go(remote(xo.at[zr, y], xs.at[zr, y], f_s.at[i], f_r.at[i], sibling))

    own_y = go(remote(xo.at[0, yh], xo.at[0, yh], y_s.at[0], y_r.at[0], across))
    up1 = go(remote(xo.at[0, yh], xo.at[3, yh], g_s.at[0], g_r.at[0], up))
    down1 = go(remote(xo.at[0, yh], xo.at[1, yh], g_s.at[1], g_r.at[1], down))
    shares = {}
    shares[0, 0] = share(0, 0, yh)
    own_y.wait_recv()
    up2 = go(remote(xo.at[0, other], xo.at[3, other], g_s.at[2], g_r.at[2], up))
    down2 = go(remote(xo.at[0, other], xo.at[1, other], g_s.at[3], g_r.at[3], down))
    shares[0, 1] = share(1, 0, other)
    up1.wait_recv()
    up3 = go(remote(xo.at[3, yh], xo.at[2, yh], g_s.at[4], g_r.at[4], up))
    shares[3, 0] = share(2, 3, yh)
    down1.wait_recv()
    shares[1, 0] = share(3, 1, yh)

    def hidden(zr):
        shares[zr, 0].wait_recv()
        shares[zr, 1].wait_recv()
        a, b = xo.at[zr], xs.at[zr]
        mine = pl.ds(pl.multiple_of(c * HALF, HALF), HALF)
        theirs = pl.ds(pl.multiple_of((1 - c) * HALF, HALF), HALF)

        def tile(n, carry):
            cols = pl.ds(pl.multiple_of(n * 256, 256), 256)
            x, y = a[...].reshape(160, HALF), b[...].reshape(160, HALF)
            g = jnp.dot(x, wg[mine, cols], preferred_element_type=F32)
            g = g + jnp.dot(y, wg[theirs, cols], preferred_element_type=F32)
            u = jnp.dot(x, wu[mine, cols], preferred_element_type=F32)
            u = u + jnp.dot(y, wu[theirs, cols], preferred_element_type=F32)
            inner[zr, :, cols] = (jax.nn.silu(g) * u).astype(BF16)
            return carry

        lax.fori_loop(0, 2, tile, 0)

    def result(zr):
        def tile(n, carry):
            cols = pl.ds(pl.multiple_of(n * 512, 512), 512)
            theirs = pl.ds(pl.multiple_of((1 - c) * HALF + n * 512, 512), 512)
            mine = pl.ds(pl.multiple_of(c * HALF + n * 512, 512), 512)
            sps[zr, :, :, cols] = (
                jnp.dot(inner[zr], wd[:, theirs], preferred_element_type=F32)
                .astype(BF16)
                .reshape(2, 80, 512)
            )
            po[zr, :, :, cols] = jnp.dot(
                inner[zr], wd[:, mine], preferred_element_type=F32
            ).reshape(2, 80, 512)
            return carry

        lax.fori_loop(0, 6, tile, 0)
        return go(remote(sps.at[zr], spr.at[zr], p_s.at[zr], p_r.at[zr], sibling))

    loads[0].wait()
    loads[1].wait()
    hidden(0)
    down2.wait_recv()
    down3 = go(remote(xo.at[1, other], xo.at[2, other], g_s.at[5], g_r.at[5], down))
    shares[1, 1] = share(4, 1, other)
    up2.wait_recv()
    shares[3, 1] = share(5, 3, other)
    loads[2].wait()
    hidden(1)
    sums = {}
    sums[1] = result(1)
    hidden(3)
    sums[3] = result(3)
    sums[0] = result(0)

    def total(zr, y):
        return po[zr, y] + spr[zr, y].astype(F32)

    sums[1].wait_recv()
    rzs[0] = total(1, other).astype(BF16)
    to_up = go(remote(rzs.at[0], rz.at[0], r_s.at[0], r_r.at[0], up))
    sums[3].wait_recv()
    rzs[1] = total(3, yh).astype(BF16)
    to_down = go(remote(rzs.at[1], rz.at[1], r_s.at[1], r_r.at[1], down))
    up3.wait_recv()
    shares[2, 0] = share(6, 2, yh)
    down3.wait_recv()
    shares[2, 1] = share(7, 2, other)
    hidden(2)
    sums[2] = result(2)
    sums[2].wait_recv()
    rzs[2] = total(2, yh).astype(BF16)
    far_up = go(remote(rzs.at[2], rz.at[2], r_s.at[2], r_r.at[2], up))
    rzs[3] = total(2, other).astype(BF16)
    far_down = go(remote(rzs.at[3], rz.at[3], r_s.at[3], r_r.at[3], down))
    far_up.wait_recv()
    rzs[4] = (total(1, yh) + rz[2].astype(F32)).astype(BF16)
    near_up = go(remote(rzs.at[4], rz.at[4], r_s.at[4], r_r.at[4], up))
    far_down.wait_recv()
    rzs[5] = (total(3, other) + rz[3].astype(F32)).astype(BF16)
    near_down = go(remote(rzs.at[5], rz.at[5], r_s.at[5], r_r.at[5], down))
    sums[0].wait_recv()
    to_up.wait_recv()
    near_down.wait_recv()
    ysend[...] = (
        total(0, other) + rz[0].astype(F32) + rz[5].astype(F32)
    ).astype(BF16)
    cross = go(remote(ysend, ry, y_s.at[1], y_r.at[1], across))
    to_down.wait_recv()
    near_up.wait_recv()
    kept = total(0, yh) + rz[1].astype(F32) + rz[4].astype(F32)
    cross.wait_recv()
    done = (kept + ry[...].astype(F32)).astype(BF16)
    bsend[...] = (
        jnp.dot(spread[...], done, preferred_element_type=F32).astype(BF16).reshape(N_REQ, TOK, HALF)
    )
    back = []
    for d in range(1, 8):
        there = (req + d) % N_REQ
        back.append(
            go(remote(bsend.at[there], ret.at[req], t_s.at[d], t_r.at[d], peers[d - 1]))
        )
    ret[req] = bsend[req]
    for cp in back:
        cp.wait_recv()
    rows = ret[...].reshape(128, HALF).astype(F32)
    msend[...] = jnp.dot(
        gates[1 - c], rows, precision=lax.Precision.HIGHEST, preferred_element_type=F32
    )
    mix = go(remote(msend, mrecv, m_s, m_r, sibling))
    ours = jnp.dot(gates[c], rows, precision=lax.Precision.HIGHEST, preferred_element_type=F32)
    mine = pl.ds(pl.multiple_of(c * HALF, HALF), HALF)
    theirs = pl.ds(pl.multiple_of((1 - c) * HALF, HALF), HALF)
    out[:, mine] = (resid[:, mine] + ours).astype(BF16)
    mix.wait_recv()
    out[:, theirs] = (resid[:, theirs] + mrecv[...]).astype(BF16)
    for cp in started:
        cp.wait_send()


def experts(packed, gates, resid, pick, spread, wg, wu, wd):
    dma = pltpu.SemaphoreType.DMA
    v = pltpu.VMEM
    return pl.pallas_call(
        expert_kernel,
        out_shape=jax.ShapeDtypeStruct((TOK, D), BF16),
        in_specs=[VMEM] * 5 + [ANY] * 3,
        out_specs=VMEM,
        scratch_shapes=[
            v((D, HID), BF16), v((D, HID), BF16), v((HID, D), BF16),
            v((N_REQ, TOK, HALF), BF16),
            v((4, 2, 80, HALF), BF16), v((4, 2, 80, HALF), BF16),
            v((4, 160, HID), BF16),
            v((4, 2, 80, HALF), F32),
            v((4, 2, 80, HALF), BF16), v((4, 2, 80, HALF), BF16),
            v((6, 80, HALF), BF16), v((6, 80, HALF), BF16),
            v((80, HALF), BF16), v((80, HALF), BF16),
            v((N_REQ, TOK, HALF), BF16), v((N_REQ, TOK, HALF), BF16),
            v((TOK, HALF), F32), v((TOK, HALF), F32),
            dma((3,)), dma((8,)), dma((8,)), dma((2,)), dma((2,)), dma((6,)), dma((6,)),
            dma((8,)), dma((8,)), dma((4,)), dma((4,)), dma((6,)), dma((6,)),
            dma((8,)), dma((8,)), dma, dma,
        ],
        name="apply_experts",
        compiler_params=pltpu.CompilerParams(
            collective_id=2, has_side_effects=True, vmem_limit_bytes=60 << 20
        ),
    )(packed, gates, resid, pick, spread, wg, wu, wd)


def tables():
    steps = np.arange(HD // 2, dtype=np.float32) / np.float32(HD // 2)
    freq = (np.float64(ROPE_BASE) ** -steps.astype(np.float64)).astype(np.float32)
    angles = (PUSE * (PLEN + GAP) + np.arange(QTOK)).astype(np.float32)[:, None] * freq[None, :]
    cosine, sine = np.cos(angles.astype(np.float64)), np.sin(angles.astype(np.float64))
    qcos = np.concatenate([cosine, cosine], axis=1).astype(np.float32)
    qsin = np.concatenate([-sine, sine], axis=1).astype(np.float32)
    pick = np.zeros((80, 128), np.float32)
    for r in range(N_REQ):
        for s in range(2 * C):
            pick[r * 2 * C + s, r * TOK + s] = 1
    return freq, qcos, qsin, pick


def per_device(
    hidden_in, queries, question_kv, passage_kv, use_lists, offsets, out_weight, norm_gain,
    router, routes, w_gate, w_up, w_down,
):
    request = lax.axis_index("req")
    core = lax.axis_index("exp") % 2
    freq, qcos, qsin, pick = tables()
    here = use_lists // PASS_DEV == request
    sel = jnp.sum(jnp.where(here, use_lists % PASS_DEV, 0), axis=1).astype(jnp.int32)
    my_uses = lax.dynamic_index_in_dim(use_lists, request, 0, keepdims=False)
    own = my_uses // PASS_DEV
    my_offsets = lax.dynamic_index_in_dim(offsets, request, 0, keepdims=False)
    p_angles = my_offsets.astype(F32)[:, None] * jnp.asarray(freq)[None, :]
    cosine, sine = jnp.cos(p_angles), jnp.sin(p_angles)
    pcos = jnp.concatenate([cosine, cosine], axis=1)
    psin = jnp.concatenate([-sine, sine], axis=1)

    expert_ids = jnp.arange(E, dtype=jnp.int32)
    flat = routes.reshape(-1)
    one_hot = (flat[:, None] == expert_ids[None, :]).astype(jnp.int32)
    ranks = jnp.sum((jnp.cumsum(one_hot, axis=0) - one_hot) * one_hot, axis=-1)
    slots = (flat * TOK + core * C + ranks).reshape(TOK, 2)
    match = slots[:, :, None] == jnp.arange(E * TOK, dtype=jnp.int32)[None, None, :]
    first, second = match[:, 0].astype(F32), match[:, 1].astype(F32)
    spots = (first + second).astype(BF16)
    named = (routes[:, :, None] == expert_ids[None, None, :]).astype(F32)
    diff = named[:, 0] - named[:, 1]

    attended = attention(
        passage_kv, queries, question_kv, sel, own, pcos, psin, jnp.asarray(qcos), jnp.asarray(qsin)
    )
    resid, packed, gates = project(
        attended.reshape(8, 2, TOK, HEADS * HD), out_weight, hidden_in, norm_gain.reshape(1, D),
        router, spots, diff, first, second,
    )
    return experts(
        packed, gates, resid, jnp.asarray(pick, BF16), jnp.asarray(pick.T, BF16),
        w_gate[0], w_up[0], w_down[0],
    )


def solution(mesh):
    in_specs = (
        P(("req", "exp"), None),
        P("req", "exp"),
        P("req", None),
        P("req", "exp", None),
        P(),
        P(),
        P("exp", "req"),
        P(),
        P(),
        P(("req", "exp"), None),
        P("req", None, "exp"),
        P("req", None, "exp"),
        P("req", "exp", None),
    )
    return jax.shard_map(
        per_device, mesh=mesh, in_specs=in_specs, out_specs=P(("req", "exp"), None), check_vma=False
    )
```

```python
import math

import jax
import jax.numpy as jnp
import numpy as np
from jax import lax
from jax.experimental import pallas as pl
from jax.experimental.pallas import tpu as pltpu
from jax.sharding import PartitionSpec as P

D = 6144
HALF = D // 2
HQ = 48
KVH = 8
HD = 128
E = 8
PLEN = 2048
PUSE = 4
PASS_DEV = 4
GAP = 64
C = 5
QTOK = 256
TOK = 16
N_REQ = 8
HID = 512
COLS = D // N_REQ
HEADS = 3
ROPE_BASE = 1000000.0
EPSILON = 1e-05
MESH = pl.DeviceIdType.MESH
F32 = jnp.float32
BF16 = jnp.bfloat16
VMEM = pl.BlockSpec(memory_space=pltpu.VMEM)
SMEM = pl.BlockSpec(memory_space=pltpu.SMEM)
ANY = pl.BlockSpec(memory_space=pl.ANY)
SCALE2 = math.log2(math.e) / math.sqrt(HD)
CHUNKS = (0, 1, 3, 2)
NCH = 4
CW = HALF // NCH


def place():
    req = lax.axis_index("req")
    exp = lax.axis_index("exp")
    return req, exp, exp // 4, (exp // 2) % 2, exp % 2


def member(z, yh, c):
    return (z * 2 + yh) * 2 + c


def remote(src, dst, send, recv, device):
    return pltpu.make_async_remote_copy(
        src_ref=src, dst_ref=dst, send_sem=send, recv_sem=recv, device_id=device, device_id_type=MESH
    )


def greet(devices):
    barrier = pltpu.get_barrier_semaphore()
    for device in devices:
        pl.semaphore_signal(barrier, inc=1, device_id=device, device_id_type=MESH)
    pl.semaphore_wait(barrier, len(devices))


def turn(vectors, cosine, sine):
    return vectors * cosine + pltpu.roll(vectors, HD // 2, vectors.ndim - 1) * sine


def loop(count, body):
    lax.fori_loop(0, count, lambda k, carry: (body(k), carry)[1], 0)


def attention_kernel(
    use_lists, offsets, pkv, q_h, qkv, qcos_h, qsin_h, pcos_h, psin_h, w_h, hid_h, gain_h, router_h,
    routes, resid_out, packed_out, gates_out,
    land0, land1, land2, land3, stage, got0, got1, got2, got3,
    kown, ksib, q_in, kvq, qcos, qsin, pcos, psin, qrot, acc, top, low,
    att, w, hid, gain, router, attb, ownp, sibs, sibr, rss, rsr, fsend, fin, nsend, nbuf, pbuf, gbuf,
    ls, s1s, s1r, s2s, s2r, fs, fr,
    a_s, a_r, b_s, b_r, c_s, c_r, d_s, d_r, e_s, e_r,
):
    req, exp, z, yh, c = place()
    x, yl = req % 4, req // 4
    chip = exp // 2
    mine = req * 2 + yh
    land = (land0, land1, land2, land3)
    got = (got0, got1, got2, got3)
    sibling = (req, member(z, yh, 1 - c))
    chips = [(req, ((chip + d) % 8) * 2 + c) for d in range(1, 8)]
    peers = [((req + d) % N_REQ, exp) for d in range(1, 8)]
    beside = ((1 - yl) * 4 + x, exp)
    right, left = (yl * 4 + (x + 1) % 4, exp), (yl * 4 + (x + 3) % 4, exp)

    loads = [
        pltpu.make_async_copy(src, dst, ls.at[i])
        for i, (src, dst) in enumerate(
            (
                (q_h, q_in),
                (qkv.at[:, pl.ds(pl.multiple_of(chip * 256, 256), 256)], kvq),
                (qcos_h, qcos), (qsin_h, qsin), (pcos_h, pcos), (psin_h, psin),
                (w_h, w), (hid_h, hid), (gain_h, gain), (router_h, router),
            )
        )
    ]
    for cp in loads:
        cp.start()

    devices = [(req, member((z + d) % 4, y, c)) for d in range(1, 4) for y in (yh, 1 - yh)]
    devices.append(sibling)
    for k in range(1, 16):
        there = (mine + k) % 16
        devices.append((there // 2, member(z, there % 2, c)))
    greet(devices)

    def cols(zt):
        return pl.ds(pl.multiple_of(zt * 512, 512), 512)

    def first(d):
        zt = (z + d) % 4
        return remote(
            pkv.at[:, :, cols(zt)], land[4 - d], s1s.at[d], s1r.at[4 - d], (req, member(zt, yh, c))
        )

    firsts = {d: first(d) for d in range(1, 4)}
    local = pltpu.make_async_copy(pkv.at[:, :, cols(z)], land0, s1r.at[0])
    local.start()
    firsts[1].start()
    firsts[3].start()

    def half(yt):
        return pl.ds(pl.multiple_of(yt * 256, 256), 256)

    def second(i, k):
        there = (mine + k) % 16
        return remote(
            stage.at[i, there // 2, :, half(there % 2)], got[i].at[mine],
            s2s.at[i, k], s2r.at[i, mine], (there // 2, member(z, there % 2, c)),
        )

    def second_in(i, k):
        there = (mine + k) % 16
        return remote(
            stage.at[i, there // 2, :, half(there % 2)], got[i].at[there],
            s2s.at[i, k], s2r.at[i, there], (there // 2, member(z, there % 2, c)),
        )

    def second_local(i):
        return pltpu.make_async_copy(
            stage.at[i, req, :, half(yh)], got[i].at[mine], s2r.at[i, mine]
        )

    sel = []
    for r in range(N_REQ):
        at = jnp.int32(0)
        for j in range(PUSE):
            p = use_lists[r, j]
            at = at + jnp.where(p // PASS_DEV == req, p % PASS_DEV, 0)
        sel.append(at)
    own = [use_lists[req, j] // PASS_DEV for j in range(PUSE)]
    spot = [
        j * GAP + jnp.clip(offsets[req, j] - j * (PLEN + GAP), 0, GAP - 1) for j in range(PUSE)
    ]

    for i, d in enumerate(CHUNKS):
        if d == 0:
            local.wait()
        else:
            firsts[4 - d].wait_recv()
        for r in range(N_REQ):
            stage[i, r] = land[d][sel[r]]
        loop(15, lambda k: second(i, k + 1).start())
        second_local(i).start()
        if i == 1:
            firsts[2].start()

        if i == 0:
            for cp in loads:
                cp.wait()
            cosine, sine = qcos[...], qsin[...]
            for h in range(HEADS):
                qrot[h * QTOK : (h + 1) * QTOK] = turn(
                    q_in[:, h * HD : (h + 1) * HD].astype(F32), cosine, sine
                ).astype(BF16)
            keys = turn(kvq[:, :HD].astype(F32), cosine, sine).astype(BF16)
            s = lax.dot_general(
                qrot[...], keys, (((1,), (1,)), ((), ())), preferred_element_type=F32
            )
            row = lax.broadcasted_iota(jnp.int32, s.shape, 0) % QTOK
            col = lax.broadcasted_iota(jnp.int32, s.shape, 1)
            s = jnp.where(col <= row, s, -jnp.inf)
            t = jnp.max(s, axis=-1, keepdims=True)
            p = jnp.exp2(s * SCALE2 - t * SCALE2)
            top[...] = jnp.broadcast_to(t, top.shape)
            low[...] = jnp.broadcast_to(jnp.sum(p, axis=-1, keepdims=True), low.shape)
            acc[...] = jnp.dot(p.astype(BF16), kvq[:, HD:], preferred_element_type=F32)

    def attend(block):
        s = lax.dot_general(
            qrot[...], block[:, :HD], (((1,), (1,)), ((), ())), preferred_element_type=F32
        )
        before = top[:, :1]
        t = jnp.maximum(before, jnp.max(s, axis=-1, keepdims=True))
        p = jnp.exp2(s * SCALE2 - t * SCALE2)
        alpha = jnp.exp2((before - t) * SCALE2)
        top[...] = jnp.broadcast_to(t, top.shape)
        low[...] = low[...] * alpha + jnp.sum(p, axis=-1, keepdims=True)
        acc[...] = acc[...] * alpha + jnp.dot(
            p.astype(BF16), block[:, HD:], preferred_element_type=F32
        )

    passes = []
    for i in range(4):
        loop(15, lambda k: second_in(i, k + 1).wait_recv())
        second_local(i).wait()
        for j in range(PUSE):
            cosine, sine = pcos[pl.ds(spot[j], 1), :], psin[pl.ds(spot[j], 1), :]
            for y in range(2):
                kv = got[i][own[j] * 2 + y]
                rows = pl.ds(j * 256 + y * 128, 128)
                kown[i, rows, :HD] = turn(kv[:, :HD].astype(F32), cosine, sine).astype(BF16)
                kown[i, rows, HD:] = kv[:, HD:]
        cp = remote(kown.at[i], ksib.at[i], fs.at[i], fr.at[i], sibling)
        cp.start()
        passes.append(cp)
        attend(kown.at[i])
        cp.wait_recv()
        attend(ksib.at[i])

    for h in range(HEADS):
        rows = pl.ds(h * QTOK, QTOK)
        att[:, :, :, h * HD : (h + 1) * HD] = (
            (acc[rows, :] / low[rows, :]).astype(BF16).reshape(8, 2, TOK, HD)
        )

    def gather(i, src, xr, side, device):
        cp = remote(src, attb.at[xr, side], a_s.at[i], a_r.at[i], device)
        cp.start()
        return cp

    swap = gather(0, att, 0, 1, beside)
    right0 = gather(1, att, 3, 0, right)
    left0 = gather(2, att, 1, 0, left)

    def multiply(k, source):
        theirs = source[:, 1 - c].reshape(128, 384)
        sibs[k] = jnp.dot(theirs, w[...], preferred_element_type=F32).astype(BF16).reshape(8, TOK, COLS)
        cp = remote(sibs.at[k], sibr.at[k], b_s.at[k], b_r.at[k], sibling)
        cp.start()
        ours = source[:, c].reshape(128, 384)
        ownp[k] = jnp.dot(ours, w[...], preferred_element_type=F32).reshape(8, TOK, COLS)
        return cp

    def scatter(k, cp):
        cp.wait_recv()
        rss[k] = (ownp[k] + sibr[k].astype(F32)).astype(BF16)
        rsr[k, chip] = rss[k, chip]
        copies = []
        for d in range(1, 8):
            there = (chip + d) % 8
            cp = remote(rss.at[k, there], rsr.at[k, chip], c_s.at[k, d], c_r.at[k, d], chips[d - 1])
            cp.start()
            copies.append(cp)
        return copies

    order = ((0, 0), (0, 1), (3, 0), (1, 0), (1, 1), (3, 1), (2, 0), (2, 1))

    def finish(k, copies):
        for cp in copies:
            cp.wait_recv()
        total = jnp.sum(rsr[k].astype(F32), axis=0).astype(BF16)
        if k == 0:
            fin[req] = total
            return None
        fsend[k] = total
        xr, side = order[k]
        target = (jnp.abs(yl - side) * 4 + (x + xr) % 4, exp)
        cp = remote(fsend.at[k], fin.at[req], d_s.at[k], d_r.at[k], target)
        cp.start()
        return cp

    halves, parts, ends, gathers = {}, {}, {}, [swap, right0, left0]
    for k in range(8 + 4):
        if k < 8:
            if k == 1:
                swap.wait_recv()
                right1 = gather(3, attb.at[0, 1], 3, 1, right)
                left1 = gather(4, attb.at[0, 1], 1, 1, left)
                right0.wait_recv()
                right2 = gather(5, attb.at[3, 0], 2, 0, right)
                gathers += [right1, left1, right2]
            elif k == 3:
                left0.wait_recv()
            elif k == 4:
                left1.wait_recv()
                left2 = gather(6, attb.at[1, 1], 2, 1, left)
                gathers.append(left2)
            elif k == 5:
                right1.wait_recv()
            elif k == 6:
                right2.wait_recv()
            elif k == 7:
                left2.wait_recv()
            halves[k] = multiply(k, att if k == 0 else attb.at[order[k][0], order[k][1]])
        if 0 <= k - 1 < 8:
            parts[k - 1] = scatter(k - 1, halves[k - 1])
        if 0 <= k - 4 < 8:
            ends[k - 4] = finish(k - 4, parts[k - 4])
    for k in range(1, 8):
        ends[k].wait_recv()

    attn = jnp.concatenate([fin[i] for i in range(N_REQ)], axis=1).astype(F32)
    resid = hid[...].astype(F32) + attn
    resid_out[...] = resid
    mean = jnp.mean(resid * resid, axis=-1, keepdims=True)
    normed = (resid * lax.rsqrt(mean + EPSILON) * gain[...]).astype(BF16)
    left_half, right_half = normed[:, :HALF], normed[:, HALF:]
    nsend[...] = jnp.where(c == 0, right_half, left_half)
    nbuf[c] = jnp.where(c == 0, left_half, right_half)
    lasts = [remote(nsend, nbuf.at[c], e_s.at[0], e_r.at[0], sibling)]
    lasts[0].start()

    row = lax.broadcasted_iota(jnp.int32, (TOK, TOK), 0)
    col = lax.broadcasted_iota(jnp.int32, (TOK, TOK), 1)
    named = lax.broadcasted_iota(jnp.int32, (TOK, E), 1)
    places = lax.broadcasted_iota(jnp.int32, (TOK, 128), 1)
    choice, hits = [], []
    for k in range(2):
        expert = jnp.sum(jnp.where(row == col, routes[k : k + 1, :], 0), axis=1, keepdims=True)
        choice.append(expert)
        hits.append((named == expert).astype(F32))
    earlier = jnp.dot(
        (col < row).astype(BF16), (hits[0] + hits[1]).astype(BF16), preferred_element_type=F32
    )
    matches = []
    for k in range(2):
        rank = jnp.sum(hits[k] * earlier, axis=1, keepdims=True).astype(jnp.int32)
        matches.append((places == choice[k] * TOK + c * C + rank).astype(F32))
    pbuf[c] = (matches[0] + matches[1]).astype(BF16)
    logits = lax.dot_general(
        normed, router[...], (((1,), (1,)), ((), ())), preferred_element_type=F32
    )
    apart = jnp.sum(logits * (hits[0] - hits[1]), axis=-1, keepdims=True)
    gates = matches[0] * jax.nn.sigmoid(apart) + matches[1] * jax.nn.sigmoid(-apart)
    coarse = gates.astype(BF16)
    gbuf[c, 0] = coarse
    gbuf[c, 1] = (gates - coarse.astype(F32)).astype(BF16)
    for i, ref in ((1, pbuf), (2, gbuf)):
        cp = remote(ref.at[c], ref.at[c], e_s.at[i], e_r.at[i], sibling)
        cp.start()
        lasts.append(cp)
    lasts[0].wait_recv()
    lasts[1].wait_recv()
    packed_out[...] = (
        lax.dot_general(
            pbuf[...].reshape(32, 128), nbuf[...].reshape(32, HALF), (((0,), (0,)), ((), ())),
            preferred_element_type=F32,
        )
        .astype(BF16)
        .reshape(E, TOK, HALF)
    )
    lasts[2].wait_recv()
    gates_out[...] = gbuf[...]

    for cp in list(firsts.values()) + passes + gathers + lasts:
        cp.wait_send()
    for i in range(4):
        loop(15, lambda k: second(i, k + 1).wait_send())
    for k in range(8):
        halves[k].wait_send()
        for cp in parts[k]:
            cp.wait_send()
        if k > 0:
            ends[k].wait_send()


def attention(*operands):
    dma = pltpu.SemaphoreType.DMA
    v = pltpu.VMEM
    return pl.pallas_call(
        attention_kernel,
        out_shape=(
            jax.ShapeDtypeStruct((TOK, D), F32),
            jax.ShapeDtypeStruct((E, TOK, HALF), BF16),
            jax.ShapeDtypeStruct((2, 2, TOK, 128), BF16),
        ),
        in_specs=[SMEM, SMEM] + [ANY] * 11 + [VMEM],
        out_specs=(VMEM,) * 3,
        scratch_shapes=[v((PASS_DEV, 128, 512), BF16)] * 4
        + [v((4, N_REQ, 128, 512), BF16)]
        + [v((16, 128, 256), BF16)] * 4
        + [
            v((4, 1024, 256), BF16), v((4, 1024, 256), BF16),
            v((QTOK, HEADS * HD), BF16), v((QTOK, 256), BF16),
            v((QTOK, HD), F32), v((QTOK, HD), F32),
            v((PUSE * GAP, HD), F32), v((PUSE * GAP, HD), F32),
            v((HEADS * QTOK, HD), BF16),
            v((HEADS * QTOK, HD), F32), v((HEADS * QTOK, HD), F32), v((HEADS * QTOK, HD), F32),
            v((8, 2, TOK, 384), BF16), v((384, COLS), BF16), v((TOK, D), BF16), v((1, D), F32),
            v((E, D), BF16), v((4, 2, 8, 2, TOK, 384), BF16),
            v((8, 8, TOK, COLS), F32),
            v((8, 8, TOK, COLS), BF16), v((8, 8, TOK, COLS), BF16),
            v((8, 8, TOK, COLS), BF16), v((8, 8, TOK, COLS), BF16),
            v((8, TOK, COLS), BF16), v((8, TOK, COLS), BF16),
            v((TOK, HALF), BF16), v((2, TOK, HALF), BF16),
            v((2, TOK, 128), BF16), v((2, 2, TOK, 128), BF16),
            dma((10,)), dma((4,)), dma((4,)), dma((4, 16)), dma((4, 16)), dma((4,)), dma((4,)),
            dma((7,)), dma((7,)), dma((8,)), dma((8,)), dma((8, 8)), dma((8, 8)),
            dma((8,)), dma((8,)), dma((3,)), dma((3,)),
        ],
        name="attend_and_project",
        compiler_params=pltpu.CompilerParams(
            collective_id=0, has_side_effects=True, vmem_limit_bytes=56 << 20
        ),
    )(*operands)


def expert_kernel(
    packed, gates, resid, wg_h, wu_h, wd_h, out,
    wg, wu, wd, prx, xo, xs, gu, inner, po, sps, spr, rzs, rz, ysend, ry, kept, bsend, ret,
    mixed, mrecv,
    w_s, a_s, a_r, y_s, y_r, g_s, g_r, f_s, f_r, p_s, p_r, r_s, r_r, t_s, t_r, m_s, m_r,
):
    req, exp, z, yh, c = place()
    other = 1 - yh
    sibling = (req, member(z, yh, 1 - c))
    across = (req, member(z, other, c))
    up = (req, member((z + 1) % 4, yh, c))
    down = (req, member((z + 3) % 4, yh, c))
    peers = [((req + d) % N_REQ, exp) for d in range(1, 8)]
    loads = [
        pltpu.make_async_copy(src, dst, w_s.at[i])
        for i, (src, dst) in enumerate(((wg_h, wg), (wu_h, wu), (wd_h, wd)))
    ]
    for cp in loads:
        cp.start()
    greet(peers + [sibling, across, up, down])

    started = []

    def go(cp):
        cp.start()
        started.append(cp)
        return cp

    def part(i):
        return pl.ds(i * CW, CW)

    row = lax.broadcasted_iota(jnp.int32, (80, 128), 0)
    col = lax.broadcasted_iota(jnp.int32, (80, 128), 1)
    pick = (col == row // 10 * TOK + row % 10).astype(BF16)
    row = lax.broadcasted_iota(jnp.int32, (128, 80), 1)
    col = lax.broadcasted_iota(jnp.int32, (128, 80), 0)
    spread = (col == row // 10 * TOK + row % 10).astype(BF16)

    arrive = []
    for i in range(NCH):
        copies = []
        for d in range(1, 8):
            there = (req + d) % N_REQ
            copies.append(
                go(remote(
                    packed.at[there, :, part(i)], prx.at[i, req], a_s.at[i, d], a_r.at[i, d], peers[d - 1]
                ))
            )
        prx[i, req] = packed[req, :, i * CW : (i + 1) * CW]
        arrive.append(copies)

    def ring(n, i, src_at, dst_at, device):
        return go(remote(
            xo.at[(i,) + src_at], xo.at[(i,) + dst_at], g_s.at[n, i], g_r.at[n, i], device
        ))

    shares = {}

    def share(i, zr, y, second):
        at = zr * 2 + second
        shares[i, zr, second] = go(remote(
            xo.at[i, zr, y], xs.at[i, zr, y], f_s.at[at, i], f_r.at[at, i], sibling
        ))

    swap, up1, down1, up2, down2, up3, down3 = {}, {}, {}, {}, {}, {}, {}
    for i in range(NCH):
        for cp in arrive[i]:
            cp.wait_recv()
        xo[i, 0, yh] = jnp.dot(
            pick, prx[i].reshape(128, CW), preferred_element_type=F32
        ).astype(BF16)
        swap[i] = ring(0, i, (0, yh), (0, yh), across)
        up1[i] = ring(1, i, (0, yh), (3, yh), up)
        down1[i] = ring(2, i, (0, yh), (1, yh), down)
        share(i, 0, yh, 0)
    for i in range(NCH):
        swap[i].wait_recv()
        up2[i] = ring(3, i, (0, other), (3, other), up)
        down2[i] = ring(4, i, (0, other), (1, other), down)
        share(i, 0, other, 1)
        up1[i].wait_recv()
        up3[i] = ring(5, i, (3, yh), (2, yh), up)
        share(i, 3, yh, 0)
        down1[i].wait_recv()
        share(i, 1, yh, 0)

    def hidden(i, zr):
        shares[i, zr, 0].wait_recv()
        shares[i, zr, 1].wait_recv()
        near = pl.ds(pl.multiple_of(c * HALF + i * CW, CW), CW)
        far = pl.ds(pl.multiple_of((1 - c) * HALF + i * CW, CW), CW)
        a, b = xo[i, zr].reshape(160, CW), xs[i, zr].reshape(160, CW)
        for n, weights in enumerate((wg, wu)):
            value = jnp.dot(a, weights[near, :], preferred_element_type=F32)
            value = value + jnp.dot(b, weights[far, :], preferred_element_type=F32)
            if i > 0:
                value = value + gu[zr, n]
            gu[zr, n] = value

    sums = {}

    def result(zr):
        inner[...] = (jax.nn.silu(gu[zr, 0]) * gu[zr, 1]).astype(BF16)
        for i in range(NCH):
            near = pl.ds(pl.multiple_of(c * HALF + i * CW, CW), CW)
            far = pl.ds(pl.multiple_of((1 - c) * HALF + i * CW, CW), CW)
            sps[i, zr] = (
                jnp.dot(inner[...], wd[:, far], preferred_element_type=F32)
                .astype(BF16)
                .reshape(2, 80, CW)
            )
            sums[i, zr] = go(remote(
                sps.at[i, zr], spr.at[i, zr], p_s.at[i, zr], p_r.at[i, zr], sibling
            ))
            po[i, zr] = (
                jnp.dot(inner[...], wd[:, near], preferred_element_type=F32)
                .astype(BF16)
                .reshape(2, 80, CW)
            )

    def total(i, zr, y):
        return po[i, zr, y].astype(F32) + spr[i, zr, y].astype(F32)

    def pass_on(n, i, value, device):
        rzs[n, i] = value.astype(BF16)
        return go(remote(rzs.at[n, i], rz.at[n, i], r_s.at[n, i], r_r.at[n, i], device))

    loads[0].wait()
    loads[1].wait()
    for i in range(NCH):
        hidden(i, 0)
    for i in range(NCH):
        down2[i].wait_recv()
        down3[i] = ring(6, i, (1, other), (2, other), down)
        share(i, 1, other, 1)
        up2[i].wait_recv()
        share(i, 3, other, 1)
        hidden(i, 1)
        hidden(i, 3)
    loads[2].wait()
    result(1)
    result(3)
    to_up, to_down, far_up, far_down, near_up, near_down = {}, {}, {}, {}, {}, {}
    for i in range(NCH):
        sums[i, 1].wait_recv()
        to_up[i] = pass_on(0, i, total(i, 1, other), up)
        sums[i, 3].wait_recv()
        to_down[i] = pass_on(1, i, total(i, 3, yh), down)
    for i in range(NCH):
        up3[i].wait_recv()
        share(i, 2, yh, 0)
        down3[i].wait_recv()
        share(i, 2, other, 1)
        if i > 0:
            hidden(i - 1, 2)
    hidden(NCH - 1, 2)
    result(2)
    for i in range(NCH):
        sums[i, 2].wait_recv()
        far_up[i] = pass_on(2, i, total(i, 2, yh), up)
        far_down[i] = pass_on(3, i, total(i, 2, other), down)
    result(0)
    for i in range(NCH):
        far_up[i].wait_recv()
        near_up[i] = pass_on(4, i, total(i, 1, yh) + rz[2, i].astype(F32), up)
        far_down[i].wait_recv()
        near_down[i] = pass_on(5, i, total(i, 3, other) + rz[3, i].astype(F32), down)
    cross, back = {}, {}
    for i in range(NCH + 2):
        if i < NCH:
            sums[i, 0].wait_recv()
            to_up[i].wait_recv()
            near_down[i].wait_recv()
            ysend[i] = (
                total(i, 0, other) + rz[0, i].astype(F32) + rz[5, i].astype(F32)
            ).astype(BF16)
            cross[i] = go(remote(ysend.at[i], ry.at[i], y_s.at[i], y_r.at[i], across))
            to_down[i].wait_recv()
            near_up[i].wait_recv()
            kept[i] = total(i, 0, yh) + rz[1, i].astype(F32) + rz[4, i].astype(F32)
        if i >= 2:
            n = i - 2
            cross[n].wait_recv()
            done = (kept[n] + ry[n].astype(F32)).astype(BF16)
            bsend[n] = (
                jnp.dot(spread, done, preferred_element_type=F32)
                .astype(BF16)
                .reshape(N_REQ, TOK, CW)
            )
            copies = []
            for d in range(1, 8):
                there = (req + d) % N_REQ
                copies.append(go(remote(
                    bsend.at[n, there], ret.at[n, req], t_s.at[n, d], t_r.at[n, d], peers[d - 1]
                )))
            ret[n, req] = bsend[n, req]
            back[n] = copies
    mix = {}
    for i in range(NCH):
        for cp in back[i]:
            cp.wait_recv()
        terms = jnp.dot(
            gates[...].reshape(4 * TOK, 128), ret[i].reshape(128, CW), preferred_element_type=F32
        ).reshape(2, 2, TOK, CW)
        mixed[i] = terms[:, 0] + terms[:, 1]
        mix[i] = go(remote(mixed.at[i, 1 - c], mrecv.at[i], m_s.at[i], m_r.at[i], sibling))
        near = pl.ds(pl.multiple_of(c * HALF + i * CW, CW), CW)
        out[:, near] = (resid[:, near] + mixed[i, c]).astype(BF16)
    for i in range(NCH):
        mix[i].wait_recv()
        far = pl.ds(pl.multiple_of((1 - c) * HALF + i * CW, CW), CW)
        out[:, far] = (resid[:, far] + mrecv[i]).astype(BF16)
    for cp in started:
        cp.wait_send()


def experts(*operands):
    dma = pltpu.SemaphoreType.DMA
    v = pltpu.VMEM
    return pl.pallas_call(
        expert_kernel,
        out_shape=jax.ShapeDtypeStruct((TOK, D), BF16),
        in_specs=[VMEM] * 3 + [ANY] * 3,
        out_specs=VMEM,
        scratch_shapes=[
            v((D, HID), BF16), v((D, HID), BF16), v((HID, D), BF16),
            v((NCH, N_REQ, TOK, CW), BF16),
            v((NCH, 4, 2, 80, CW), BF16), v((NCH, 4, 2, 80, CW), BF16),
            v((4, 2, 160, HID), F32),
            v((160, HID), BF16),
            v((NCH, 4, 2, 80, CW), BF16), v((NCH, 4, 2, 80, CW), BF16), v((NCH, 4, 2, 80, CW), BF16),
            v((6, NCH, 80, CW), BF16), v((6, NCH, 80, CW), BF16),
            v((NCH, 80, CW), BF16), v((NCH, 80, CW), BF16), v((NCH, 80, CW), F32),
            v((NCH, N_REQ, TOK, CW), BF16), v((NCH, N_REQ, TOK, CW), BF16),
            v((NCH, 2, TOK, CW), F32), v((NCH, TOK, CW), F32),
            dma((3,)), dma((NCH, 8)), dma((NCH, 8)), dma((NCH,)), dma((NCH,)),
            dma((7, NCH)), dma((7, NCH)), dma((8, NCH)), dma((8, NCH)),
            dma((NCH, 4)), dma((NCH, 4)), dma((6, NCH)), dma((6, NCH)),
            dma((NCH, 8)), dma((NCH, 8)), dma((NCH,)), dma((NCH,)),
        ],
        name="apply_experts",
        compiler_params=pltpu.CompilerParams(
            collective_id=1, has_side_effects=True, vmem_limit_bytes=60 << 20
        ),
    )(*operands)


def rotation(positions):
    steps = np.arange(HD // 2, dtype=np.float32) / np.float32(HD // 2)
    freq = (np.float64(ROPE_BASE) ** -steps.astype(np.float64)).astype(np.float32)
    angles = positions.astype(np.float32)[:, None] * freq[None, :]
    cosine, sine = np.cos(angles.astype(np.float64)), np.sin(angles.astype(np.float64))
    return (
        jnp.asarray(np.concatenate([cosine, cosine], axis=1), F32),
        jnp.asarray(np.concatenate([-sine, sine], axis=1), F32),
    )


def per_device(
    hidden_in, queries, question_kv, passage_kv, use_lists, offsets, out_weight, norm_gain,
    router, routes, w_gate, w_up, w_down,
):
    qcos, qsin = rotation(PUSE * (PLEN + GAP) + np.arange(QTOK))
    starts = np.arange(PUSE)[:, None] * (PLEN + GAP) + np.arange(GAP)[None, :]
    pcos, psin = rotation(starts.reshape(-1))
    resid, packed, gates = attention(
        use_lists, offsets, passage_kv, queries, question_kv, qcos, qsin, pcos, psin, out_weight,
        hidden_in, norm_gain.reshape(1, D), router.T, routes.T,
    )
    return experts(packed, gates, resid, w_gate[0], w_up[0], w_down[0])


def solution(mesh):
    in_specs = (
        P(("req", "exp"), None),
        P("req", "exp"),
        P("req", None),
        P("req", "exp", None),
        P(),
        P(),
        P("exp", "req"),
        P(),
        P(),
        P(("req", "exp"), None),
        P("req", None, "exp"),
        P("req", None, "exp"),
        P("req", "exp", None),
    )
    return jax.shard_map(
        per_device, mesh=mesh, in_specs=in_specs, out_specs=P(("req", "exp"), None), check_vma=False
    )
```

```python
import math

import jax
import jax.numpy as jnp
import numpy as np
from jax import lax
from jax.experimental import pallas as pl
from jax.experimental.pallas import tpu as pltpu
from jax.sharding import PartitionSpec as P

D = 6144
HALF = D // 2
HQ = 48
KVH = 8
HD = 128
E = 8
PLEN = 2048
PUSE = 4
PASS_DEV = 4
GAP = 64
C = 5
QTOK = 256
TOK = 16
N_REQ = 8
HID = 512
COLS = D // N_REQ
HEADS = 3
ROPE_BASE = 1000000.0
EPSILON = 1e-05
MESH = pl.DeviceIdType.MESH
F32 = jnp.float32
BF16 = jnp.bfloat16
VMEM = pl.BlockSpec(memory_space=pltpu.VMEM)
SMEM = pl.BlockSpec(memory_space=pltpu.SMEM)
ANY = pl.BlockSpec(memory_space=pl.ANY)
SCALE2 = math.log2(math.e) / math.sqrt(HD)
CHUNKS = (0, 1, 3, 2)
LATE = (0,)
NCH = 3
CW = HALF // NCH
CUT = CW // 2


def place():
    req = lax.axis_index("req")
    exp = lax.axis_index("exp")
    return req, exp, exp // 4, (exp // 2) % 2, exp % 2


def member(z, yh, c):
    return (z * 2 + yh) * 2 + c


def remote(src, dst, send, recv, device):
    return pltpu.make_async_remote_copy(
        src_ref=src, dst_ref=dst, send_sem=send, recv_sem=recv, device_id=device, device_id_type=MESH
    )


def greet(devices):
    barrier = pltpu.get_barrier_semaphore()
    for device in devices:
        pl.semaphore_signal(barrier, inc=1, device_id=device, device_id_type=MESH)
    pl.semaphore_wait(barrier, len(devices))


def turn(vectors, cosine, sine):
    return vectors * cosine + pltpu.roll(vectors, HD // 2, vectors.ndim - 1) * sine


def loop(count, body):
    lax.fori_loop(0, count, lambda k, carry: (body(k), carry)[1], 0)


def attention_kernel(
    table, pkv, q_h, qkv, qcos_h, qsin_h, pcos_h, psin_h, w_h, hid_h, gain_h, router_h,
    routes, resid_out, packed_out, gates_out,
    land0, land1, land2, land3, stage, got0, got1, got2, got3,
    kown, ksib, q_in, kvq, qcos, qsin, pcos, psin, qrot, acc, top, low,
    att, w, hid, gain, router, attb, ownp, sibs, sibr, rss, rsr, fsend, fin, nsend, nbuf, pbuf, gbuf,
    ls, s1s, s1r, s2s, s2r, fs, fr,
    a_s, a_r, b_s, b_r, c_s, c_r, d_s, d_r, e_s, e_r,
):
    req, exp, z, yh, c = place()
    x, yl = req % 4, req // 4
    chip = exp // 2
    mine = req * 2 + yh
    land = (land0, land1, land2, land3)
    got = (got0, got1, got2, got3)
    sibling = (req, member(z, yh, 1 - c))
    chips = [(req, ((chip + d) % 8) * 2 + c) for d in range(1, 8)]
    peers = [((req + d) % N_REQ, exp) for d in range(1, 8)]
    beside = ((1 - yl) * 4 + x, exp)
    right, left = (yl * 4 + (x + 1) % 4, exp), (yl * 4 + (x + 3) % 4, exp)

    loads = [
        pltpu.make_async_copy(src, dst, ls.at[i])
        for i, (src, dst) in enumerate(
            (
                (q_h, q_in),
                (qkv.at[:, pl.ds(pl.multiple_of(chip * 256, 256), 256)], kvq),
                (qcos_h, qcos), (qsin_h, qsin), (pcos_h, pcos), (psin_h, psin),
                (w_h, w), (hid_h, hid), (gain_h, gain), (router_h, router),
            )
        )
    ]
    for cp in loads:
        cp.start()

    devices = [(req, member((z + d) % 4, y, c)) for d in range(1, 4) for y in (yh, 1 - yh)]
    devices.append(sibling)
    for k in range(1, 16):
        there = (mine + k) % 16
        devices.append((there // 2, member(z, there % 2, c)))
    greet(devices)

    def cols(zt):
        return pl.ds(pl.multiple_of(zt * 512, 512), 512)

    def first(d):
        zt = (z + d) % 4
        return remote(
            pkv.at[:, :, cols(zt)], land[4 - d], s1s.at[d], s1r.at[4 - d], (req, member(zt, yh, c))
        )

    firsts = {d: first(d) for d in range(1, 4)}
    local = pltpu.make_async_copy(pkv.at[:, :, cols(z)], land0, s1r.at[0])
    local.start()
    firsts[1].start()
    firsts[3].start()

    def half(yt):
        return pl.ds(pl.multiple_of(yt * 256, 256), 256)

    def second(i, k):
        there = (mine + k) % 16
        return remote(
            stage.at[i, there // 2, :, half(there % 2)], got[i].at[mine],
            s2s.at[i, k], s2r.at[i, mine], (there // 2, member(z, there % 2, c)),
        )

    def second_in(i, k):
        there = (mine + k) % 16
        return remote(
            stage.at[i, there // 2, :, half(there % 2)], got[i].at[there],
            s2s.at[i, k], s2r.at[i, there], (there // 2, member(z, there % 2, c)),
        )

    def second_local(i):
        return pltpu.make_async_copy(
            stage.at[i, req, :, half(yh)], got[i].at[mine], s2r.at[i, mine]
        )

    sel = []
    for r in range(N_REQ):
        at = jnp.int32(0)
        for j in range(PUSE):
            p = table[r, j]
            at = at + jnp.where(p // PASS_DEV == req, p % PASS_DEV, 0)
        sel.append(at)
    own = [table[req, j] // PASS_DEV for j in range(PUSE)]
    spot = [
        j * GAP + jnp.clip(table[req, PUSE + j] - j * (PLEN + GAP), 0, GAP - 1) for j in range(PUSE)
    ]

    for i, d in enumerate(CHUNKS):
        if d == 0:
            local.wait()
        else:
            firsts[4 - d].wait_recv()
        for r in range(N_REQ):
            stage[i, r] = land[d][sel[r]]
        loop(15, lambda k: second(i, k + 1).start())
        second_local(i).start()
        if i == 1:
            firsts[2].start()

        if i == 0:
            for cp in loads:
                cp.wait()
            cosine, sine = qcos[...], qsin[...]
            for h in range(HEADS):
                qrot[h * QTOK : (h + 1) * QTOK] = turn(
                    q_in[:, h * HD : (h + 1) * HD].astype(F32), cosine, sine
                ).astype(BF16)
            keys = turn(kvq[:, :HD].astype(F32), cosine, sine).astype(BF16)
            s = lax.dot_general(
                qrot[...], keys, (((1,), (1,)), ((), ())), preferred_element_type=F32
            )
            row = lax.broadcasted_iota(jnp.int32, s.shape, 0) % QTOK
            col = lax.broadcasted_iota(jnp.int32, s.shape, 1)
            s = jnp.where(col <= row, s, -jnp.inf)
            t = jnp.max(s, axis=-1, keepdims=True)
            p = jnp.exp2(s * SCALE2 - t * SCALE2)
            top[...] = jnp.broadcast_to(t, top.shape)
            low[...] = jnp.broadcast_to(jnp.sum(p, axis=-1, keepdims=True), low.shape)
            acc[...] = jnp.dot(p.astype(BF16), kvq[:, HD:], preferred_element_type=F32)

    def attend(block):
        s = lax.dot_general(
            qrot[...], block[:, :HD], (((1,), (1,)), ((), ())), preferred_element_type=F32
        )
        before = top[:, :1]
        t = jnp.maximum(before, jnp.max(s, axis=-1, keepdims=True))
        p = jnp.exp2(s * SCALE2 - t * SCALE2)
        alpha = jnp.exp2((before - t) * SCALE2)
        top[...] = jnp.broadcast_to(t, top.shape)
        low[...] = low[...] * alpha + jnp.sum(p, axis=-1, keepdims=True)
        acc[...] = acc[...] * alpha + jnp.dot(
            p.astype(BF16), block[:, HD:], preferred_element_type=F32
        )

    passes = []
    for i in range(4):
        loop(15, lambda k: second_in(i, k + 1).wait_recv())
        second_local(i).wait()
        for j in range(PUSE):
            cosine, sine = pcos[pl.ds(spot[j], 1), :], psin[pl.ds(spot[j], 1), :]
            for y in range(2):
                kv = got[i][own[j] * 2 + y]
                rows = pl.ds(j * 256 + y * 128, 128)
                kown[i, rows, :HD] = turn(kv[:, :HD].astype(F32), cosine, sine).astype(BF16)
                kown[i, rows, HD:] = kv[:, HD:]
        cp = remote(kown.at[i], ksib.at[i], fs.at[i], fr.at[i], sibling)
        cp.start()
        passes.append(cp)
        attend(kown.at[i])
        cp.wait_recv()
        attend(ksib.at[i])

    for h in range(HEADS):
        rows = pl.ds(h * QTOK, QTOK)
        att[:, :, :, h * HD : (h + 1) * HD] = (
            (acc[rows, :] / low[rows, :]).astype(BF16).reshape(8, 2, TOK, HD)
        )

    def gather(i, src, xr, side, device):
        cp = remote(src, attb.at[xr, side], a_s.at[i], a_r.at[i], device)
        cp.start()
        return cp

    swap = gather(0, att, 0, 1, beside)
    right0 = gather(1, att, 3, 0, right)
    left0 = gather(2, att, 1, 0, left)

    def multiply(k, source):
        theirs = source[:, 1 - c].reshape(128, 384)
        sibs[k] = jnp.dot(theirs, w[...], preferred_element_type=F32).astype(BF16).reshape(8, TOK, COLS)
        cp = remote(sibs.at[k], sibr.at[k], b_s.at[k], b_r.at[k], sibling)
        cp.start()
        ours = source[:, c].reshape(128, 384)
        ownp[k] = jnp.dot(ours, w[...], preferred_element_type=F32).reshape(8, TOK, COLS)
        return cp

    def scatter(k, cp):
        cp.wait_recv()
        rss[k] = (ownp[k] + sibr[k].astype(F32)).astype(BF16)
        rsr[k, chip] = rss[k, chip]
        copies = []
        for d in range(1, 8):
            there = (chip + d) % 8
            cp = remote(rss.at[k, there], rsr.at[k, chip], c_s.at[k, d], c_r.at[k, d], chips[d - 1])
            cp.start()
            copies.append(cp)
        return copies

    order = ((0, 0), (0, 1), (3, 0), (1, 0), (1, 1), (3, 1), (2, 0), (2, 1))

    def finish(k, copies):
        for cp in copies:
            cp.wait_recv()
        total = jnp.sum(rsr[k].astype(F32), axis=0).astype(BF16)
        if k == 0:
            fin[req] = total
            return None
        fsend[k] = total
        xr, side = order[k]
        target = (jnp.abs(yl - side) * 4 + (x + xr) % 4, exp)
        cp = remote(fsend.at[k], fin.at[req], d_s.at[k], d_r.at[k], target)
        cp.start()
        return cp

    halves, parts, ends, gathers = {}, {}, {}, [swap, right0, left0]
    for k in range(8 + 4):
        if k < 8:
            if k == 1:
                swap.wait_recv()
                right1 = gather(3, attb.at[0, 1], 3, 1, right)
                left1 = gather(4, attb.at[0, 1], 1, 1, left)
                right0.wait_recv()
                right2 = gather(5, attb.at[3, 0], 2, 0, right)
                gathers += [right1, left1, right2]
            elif k == 3:
                left0.wait_recv()
            elif k == 4:
                left1.wait_recv()
                left2 = gather(6, attb.at[1, 1], 2, 1, left)
                gathers.append(left2)
            elif k == 5:
                right1.wait_recv()
            elif k == 6:
                right2.wait_recv()
            elif k == 7:
                left2.wait_recv()
            halves[k] = multiply(k, att if k == 0 else attb.at[order[k][0], order[k][1]])
        if 0 <= k - 1 < 8:
            parts[k - 1] = scatter(k - 1, halves[k - 1])
        if 0 <= k - 4 < 8:
            ends[k - 4] = finish(k - 4, parts[k - 4])
    for k in range(1, 8):
        ends[k].wait_recv()

    attn = jnp.concatenate([fin[i] for i in range(N_REQ)], axis=1).astype(F32)
    resid = hid[...].astype(F32) + attn
    resid_out[...] = resid
    mean = jnp.mean(resid * resid, axis=-1, keepdims=True)
    normed = (resid * lax.rsqrt(mean + EPSILON) * gain[...]).astype(BF16)
    left_half, right_half = normed[:, :HALF], normed[:, HALF:]
    nsend[...] = jnp.where(c == 0, right_half, left_half)
    nbuf[c] = jnp.where(c == 0, left_half, right_half)
    lasts = [remote(nsend, nbuf.at[c], e_s.at[0], e_r.at[0], sibling)]
    lasts[0].start()

    row = lax.broadcasted_iota(jnp.int32, (TOK, TOK), 0)
    col = lax.broadcasted_iota(jnp.int32, (TOK, TOK), 1)
    named = lax.broadcasted_iota(jnp.int32, (TOK, E), 1)
    places = lax.broadcasted_iota(jnp.int32, (TOK, 128), 1)
    choice, hits = [], []
    for k in range(2):
        expert = jnp.sum(jnp.where(row == col, routes[k : k + 1, :], 0), axis=1, keepdims=True)
        choice.append(expert)
        hits.append((named == expert).astype(F32))
    earlier = jnp.dot(
        (col < row).astype(BF16), (hits[0] + hits[1]).astype(BF16), preferred_element_type=F32
    )
    matches = []
    for k in range(2):
        rank = jnp.sum(hits[k] * earlier, axis=1, keepdims=True).astype(jnp.int32)
        matches.append((places == choice[k] * TOK + c * C + rank).astype(F32))
    pbuf[c] = (matches[0] + matches[1]).astype(BF16)
    logits = lax.dot_general(
        normed, router[...], (((1,), (1,)), ((), ())), preferred_element_type=F32
    )
    apart = jnp.sum(logits * (hits[0] - hits[1]), axis=-1, keepdims=True)
    gates = matches[0] * jax.nn.sigmoid(apart) + matches[1] * jax.nn.sigmoid(-apart)
    coarse = gates.astype(BF16)
    gbuf[c, 0] = coarse
    gbuf[c, 1] = (gates - coarse.astype(F32)).astype(BF16)
    for i, ref in ((1, pbuf), (2, gbuf)):
        cp = remote(ref.at[c], ref.at[c], e_s.at[i], e_r.at[i], sibling)
        cp.start()
        lasts.append(cp)
    lasts[0].wait_recv()
    lasts[1].wait_recv()
    packed_out[...] = (
        lax.dot_general(
            pbuf[...].reshape(32, 128), nbuf[...].reshape(32, HALF), (((0,), (0,)), ((), ())),
            preferred_element_type=F32,
        )
        .astype(BF16)
        .reshape(E, TOK, HALF)
    )
    lasts[2].wait_recv()
    gates_out[...] = gbuf[...]

    for cp in list(firsts.values()) + passes + gathers + lasts:
        cp.wait_send()
    for i in range(4):
        loop(15, lambda k: second(i, k + 1).wait_send())
    for k in range(8):
        halves[k].wait_send()
        for cp in parts[k]:
            cp.wait_send()
        if k > 0:
            ends[k].wait_send()


def attention(*operands):
    dma = pltpu.SemaphoreType.DMA
    v = pltpu.VMEM
    return pl.pallas_call(
        attention_kernel,
        out_shape=(
            jax.ShapeDtypeStruct((TOK, D), F32),
            jax.ShapeDtypeStruct((E, TOK, HALF), BF16),
            jax.ShapeDtypeStruct((2, 2, TOK, 128), BF16),
        ),
        in_specs=[SMEM] + [ANY] * 11 + [VMEM],
        out_specs=(VMEM,) * 3,
        scratch_shapes=[v((PASS_DEV, 128, 512), BF16)] * 4
        + [v((4, N_REQ, 128, 512), BF16)]
        + [v((16, 128, 256), BF16)] * 4
        + [
            v((4, 1024, 256), BF16), v((4, 1024, 256), BF16),
            v((QTOK, HEADS * HD), BF16), v((QTOK, 256), BF16),
            v((QTOK, HD), F32), v((QTOK, HD), F32),
            v((PUSE * GAP, HD), F32), v((PUSE * GAP, HD), F32),
            v((HEADS * QTOK, HD), BF16),
            v((HEADS * QTOK, HD), F32), v((HEADS * QTOK, HD), F32), v((HEADS * QTOK, HD), F32),
            v((8, 2, TOK, 384), BF16), v((384, COLS), BF16), v((TOK, D), BF16), v((1, D), F32),
            v((E, D), BF16), v((4, 2, 8, 2, TOK, 384), BF16),
            v((8, 8, TOK, COLS), F32),
            v((8, 8, TOK, COLS), BF16), v((8, 8, TOK, COLS), BF16),
            v((8, 8, TOK, COLS), BF16), v((8, 8, TOK, COLS), BF16),
            v((8, TOK, COLS), BF16), v((8, TOK, COLS), BF16),
            v((TOK, HALF), BF16), v((2, TOK, HALF), BF16),
            v((2, TOK, 128), BF16), v((2, 2, TOK, 128), BF16),
            dma((10,)), dma((4,)), dma((4,)), dma((4, 16)), dma((4, 16)), dma((4,)), dma((4,)),
            dma((7,)), dma((7,)), dma((8,)), dma((8,)), dma((8, 8)), dma((8, 8)),
            dma((8,)), dma((8,)), dma((3,)), dma((3,)),
        ],
        name="attend_and_project",
        compiler_params=pltpu.CompilerParams(
            collective_id=0, has_side_effects=True, vmem_limit_bytes=56 << 20
        ),
    )(*operands)


def expert_kernel(
    packed, gates, resid, wg_h, wu_h, wd_h, out,
    wg, wu, wd, prx, xo, xs, gu, inner, po, sps, spr, rzs, rz, ysend, ry, kept, bsend, ret,
    mixed, mrecv,
    w_s, a_s, a_r, y_s, y_r, g_s, g_r, f_s, f_r, p_s, p_r, r_s, r_r, t_s, t_r, m_s, m_r,
):
    req, exp, z, yh, c = place()
    other = 1 - yh
    sibling = (req, member(z, yh, 1 - c))
    across = (req, member(z, other, c))
    up = (req, member((z + 1) % 4, yh, c))
    down = (req, member((z + 3) % 4, yh, c))
    peers = [((req + d) % N_REQ, exp) for d in range(1, 8)]
    loads = [
        pltpu.make_async_copy(src, dst, w_s.at[i])
        for i, (src, dst) in enumerate(((wg_h, wg), (wu_h, wu), (wd_h, wd)))
    ]
    for cp in loads:
        cp.start()
    greet(peers + [sibling, across, up, down])

    started = []

    def go(cp):
        cp.start()
        started.append(cp)
        return cp

    def part(i):
        return pl.ds(i * CW, CW)

    row = lax.broadcasted_iota(jnp.int32, (80, 128), 0)
    col = lax.broadcasted_iota(jnp.int32, (80, 128), 1)
    pick = (col == row // 10 * TOK + row % 10).astype(BF16)
    row = lax.broadcasted_iota(jnp.int32, (128, 80), 1)
    col = lax.broadcasted_iota(jnp.int32, (128, 80), 0)
    spread = (col == row // 10 * TOK + row % 10).astype(BF16)

    arrive = []
    for i in range(NCH):
        copies = []
        for d in range(1, 8):
            there = (req + d) % N_REQ
            copies.append(
                go(remote(
                    packed.at[there, :, part(i)], prx.at[i, req], a_s.at[i, d], a_r.at[i, d], peers[d - 1]
                ))
            )
        prx[i, req] = packed[req, :, i * CW : (i + 1) * CW]
        arrive.append(copies)

    def ring(n, i, src_at, dst_at, device):
        return go(remote(
            xo.at[(i,) + src_at], xo.at[(i,) + dst_at], g_s.at[n, i], g_r.at[n, i], device
        ))

    shares = {}

    def share(i, zr, y, second):
        at = zr * 2 + second
        shares[i, zr, second] = go(remote(
            xo.at[i, zr, y], xs.at[i, zr, y], f_s.at[at, i], f_r.at[at, i], sibling
        ))

    swap, up1, down1, up2, down2, up3, down3 = {}, {}, {}, {}, {}, {}, {}
    over1, over2, over3 = {}, {}, {}
    lower, upper = (slice(None), pl.ds(0, CUT)), (slice(None), pl.ds(CUT, CUT))
    for i in range(NCH):
        for cp in arrive[i]:
            cp.wait_recv()
        xo[i, 0, yh] = jnp.dot(
            pick, prx[i].reshape(128, CW), preferred_element_type=F32
        ).astype(BF16)
        swap[i] = ring(0, i, (0, yh), (0, yh), across)
        up1[i] = ring(1, i, (0, yh), (3, yh), up)
        down1[i] = ring(2, i, (0, yh), (1, yh), down)
        share(i, 0, yh, 0)
    for i in range(NCH):
        if i in LATE:
            up1[i].wait_recv()
            up3[i] = ring(5, i, (3, yh) + lower, (2, yh) + lower, up)
            over3[i] = ring(3, i, (3, yh), (3, yh), across)
            share(i, 3, yh, 0)
            down1[i].wait_recv()
            down3[i] = ring(6, i, (1, yh) + upper, (2, yh) + upper, down)
            over1[i] = ring(4, i, (1, yh), (1, yh), across)
            share(i, 1, yh, 0)
            swap[i].wait_recv()
            share(i, 0, other, 1)
        else:
            swap[i].wait_recv()
            up2[i] = ring(3, i, (0, other), (3, other), up)
            down2[i] = ring(4, i, (0, other), (1, other), down)
            share(i, 0, other, 1)
            up1[i].wait_recv()
            up3[i] = ring(5, i, (3, yh), (2, yh), up)
            share(i, 3, yh, 0)
            down1[i].wait_recv()
            share(i, 1, yh, 0)

    def hidden(i, zr):
        shares[i, zr, 0].wait_recv()
        shares[i, zr, 1].wait_recv()
        near = pl.ds(pl.multiple_of(c * HALF + i * CW, CW), CW)
        far = pl.ds(pl.multiple_of((1 - c) * HALF + i * CW, CW), CW)
        a, b = xo[i, zr].reshape(160, CW), xs[i, zr].reshape(160, CW)
        for n, weights in enumerate((wg, wu)):
            value = jnp.dot(a, weights[near, :], preferred_element_type=F32)
            value = value + jnp.dot(b, weights[far, :], preferred_element_type=F32)
            if i > 0:
                value = value + gu[zr, n]
            gu[zr, n] = value

    sums = {}

    def result(zr):
        inner[...] = (jax.nn.silu(gu[zr, 0]) * gu[zr, 1]).astype(BF16)
        for i in range(NCH):
            near = pl.ds(pl.multiple_of(c * HALF + i * CW, CW), CW)
            far = pl.ds(pl.multiple_of((1 - c) * HALF + i * CW, CW), CW)
            sps[i, zr] = (
                jnp.dot(inner[...], wd[:, far], preferred_element_type=F32)
                .astype(BF16)
                .reshape(2, 80, CW)
            )
            sums[i, zr] = go(remote(
                sps.at[i, zr], spr.at[i, zr], p_s.at[i, zr], p_r.at[i, zr], sibling
            ))
            po[i, zr] = (
                jnp.dot(inner[...], wd[:, near], preferred_element_type=F32)
                .astype(BF16)
                .reshape(2, 80, CW)
            )

    def total(i, zr, y):
        return po[i, zr, y].astype(F32) + spr[i, zr, y].astype(F32)

    def pass_on(n, i, value, device):
        rzs[n, i] = value.astype(BF16)
        return go(remote(rzs.at[n, i], rz.at[n, i], r_s.at[n, i], r_r.at[n, i], device))

    loads[0].wait()
    loads[1].wait()
    for i in range(NCH):
        hidden(i, 0)
    for i in range(NCH):
        if i in LATE:
            up3[i].wait_recv()
            down3[i].wait_recv()
            over2[i] = ring(7, i, (2, yh), (2, yh), across)
            share(i, 2, yh, 0)
            over1[i].wait_recv()
            share(i, 1, other, 1)
            over3[i].wait_recv()
            share(i, 3, other, 1)
        else:
            down2[i].wait_recv()
            down3[i] = ring(6, i, (1, other), (2, other), down)
            share(i, 1, other, 1)
            up2[i].wait_recv()
            share(i, 3, other, 1)
        hidden(i, 1)
        hidden(i, 3)
    loads[2].wait()
    result(1)
    result(3)
    early = [i for i in range(NCH) if i not in LATE]
    to_up, to_down, far_up, far_down, near_up, near_down = {}, {}, {}, {}, {}, {}
    cross, cross1, cross2, cross3, back = {}, {}, {}, {}, {}
    for i in range(NCH):
        sums[i, 1].wait_recv()
        sums[i, 3].wait_recv()
        if i in LATE:
            cross1[i] = pass_on(0, i, total(i, 1, other), across)
            cross3[i] = pass_on(1, i, total(i, 3, other), across)
        else:
            to_up[i] = pass_on(0, i, total(i, 1, other), up)
            to_down[i] = pass_on(1, i, total(i, 3, yh), down)
    for i in range(NCH):
        if i in LATE:
            over2[i].wait_recv()
            share(i, 2, other, 1)
        else:
            up3[i].wait_recv()
            share(i, 2, yh, 0)
            down3[i].wait_recv()
            share(i, 2, other, 1)
        if i > 0:
            hidden(i - 1, 2)
    hidden(NCH - 1, 2)
    result(2)
    for i in range(NCH):
        sums[i, 2].wait_recv()
        if i in LATE:
            cross2[i] = pass_on(6, i, total(i, 2, other), across)
        else:
            far_up[i] = pass_on(2, i, total(i, 2, yh), up)
            far_down[i] = pass_on(3, i, total(i, 2, other), down)
    result(0)

    def cross_over(i, value):
        ysend[i] = value.astype(BF16)
        cross[i] = go(remote(ysend.at[i], ry.at[i], y_s.at[i], y_r.at[i], across))

    for i in LATE:
        sums[i, 0].wait_recv()
        cross_over(i, total(i, 0, other))
        cross2[i].wait_recv()
        both = (total(i, 2, yh) + rz[6, i].astype(F32)).astype(BF16)
        rzs[2, i, :, :CUT] = both[:, :CUT]
        rzs[3, i, :, CUT:] = both[:, CUT:]
        for n, cols, device, copies in ((2, lower, up, far_up), (3, upper, down, far_down)):
            copies[i] = go(remote(
                rzs.at[(n, i) + cols], rz.at[(n, i) + cols], r_s.at[n, i], r_r.at[n, i], device
            ))
    for i in early:
        far_up[i].wait_recv()
        near_up[i] = pass_on(4, i, total(i, 1, yh) + rz[2, i].astype(F32), up)
        far_down[i].wait_recv()
        near_down[i] = pass_on(5, i, total(i, 3, other) + rz[3, i].astype(F32), down)
    for i in LATE:
        cross1[i].wait_recv()
        cross3[i].wait_recv()
        far_up[i].wait_recv()
        far_down[i].wait_recv()
        ahead = total(i, 1, yh) + rz[0, i].astype(F32)
        behind = total(i, 3, yh) + rz[1, i].astype(F32)
        added = jnp.concatenate(
            [ahead[:, :CUT] + rz[2, i, :, :CUT].astype(F32), ahead[:, CUT:]], axis=1
        )
        near_up[i] = pass_on(4, i, added, up)
        added = jnp.concatenate(
            [behind[:, :CUT], behind[:, CUT:] + rz[3, i, :, CUT:].astype(F32)], axis=1
        )
        near_down[i] = pass_on(5, i, added, down)

    def gathered(i):
        sums[i, 0].wait_recv()
        to_up[i].wait_recv()
        near_down[i].wait_recv()
        cross_over(i, total(i, 0, other) + rz[0, i].astype(F32) + rz[5, i].astype(F32))
        to_down[i].wait_recv()
        near_up[i].wait_recv()
        kept[i] = total(i, 0, yh) + rz[1, i].astype(F32) + rz[4, i].astype(F32)

    def give_back(i):
        cross[i].wait_recv()
        done = kept[i] + ry[i].astype(F32)
        if i in LATE:
            near_up[i].wait_recv()
            near_down[i].wait_recv()
            done = done + rz[4, i].astype(F32) + rz[5, i].astype(F32)
        bsend[i] = (
            jnp.dot(spread, done.astype(BF16), preferred_element_type=F32)
            .astype(BF16)
            .reshape(N_REQ, TOK, CW)
        )
        copies = []
        for d in range(1, 8):
            there = (req + d) % N_REQ
            copies.append(go(remote(
                bsend.at[i, there], ret.at[i, req], t_s.at[i, d], t_r.at[i, d], peers[d - 1]
            )))
        ret[i, req] = bsend[i, req]
        back[i] = copies

    for i in LATE:
        kept[i] = total(i, 0, yh)
    gathered(early[0])
    for n in range(1, len(early)):
        gathered(early[n])
        give_back(early[n - 1])
    give_back(early[-1])
    for i in LATE:
        give_back(i)
    mix = {}
    for i in early + list(LATE):
        for cp in back[i]:
            cp.wait_recv()
        terms = jnp.dot(
            gates[...].reshape(4 * TOK, 128), ret[i].reshape(128, CW), preferred_element_type=F32
        ).reshape(2, 2, TOK, CW)
        mixed[i] = terms[:, 0] + terms[:, 1]
        mix[i] = go(remote(mixed.at[i, 1 - c], mrecv.at[i], m_s.at[i], m_r.at[i], sibling))
        near = pl.ds(pl.multiple_of(c * HALF + i * CW, CW), CW)
        out[:, near] = (resid[:, near] + mixed[i, c]).astype(BF16)
    for i in early + list(LATE):
        mix[i].wait_recv()
        far = pl.ds(pl.multiple_of((1 - c) * HALF + i * CW, CW), CW)
        out[:, far] = (resid[:, far] + mrecv[i]).astype(BF16)
    for cp in started:
        cp.wait_send()


def experts(*operands):
    dma = pltpu.SemaphoreType.DMA
    v = pltpu.VMEM
    return pl.pallas_call(
        expert_kernel,
        out_shape=jax.ShapeDtypeStruct((TOK, D), BF16),
        in_specs=[VMEM] * 3 + [ANY] * 3,
        out_specs=VMEM,
        scratch_shapes=[
            v((D, HID), BF16), v((D, HID), BF16), v((HID, D), BF16),
            v((NCH, N_REQ, TOK, CW), BF16),
            v((NCH, 4, 2, 80, CW), BF16), v((NCH, 4, 2, 80, CW), BF16),
            v((4, 2, 160, HID), F32),
            v((160, HID), BF16),
            v((NCH, 4, 2, 80, CW), BF16), v((NCH, 4, 2, 80, CW), BF16), v((NCH, 4, 2, 80, CW), BF16),
            v((7, NCH, 80, CW), BF16), v((7, NCH, 80, CW), BF16),
            v((NCH, 80, CW), BF16), v((NCH, 80, CW), BF16), v((NCH, 80, CW), F32),
            v((NCH, N_REQ, TOK, CW), BF16), v((NCH, N_REQ, TOK, CW), BF16),
            v((NCH, 2, TOK, CW), F32), v((NCH, TOK, CW), F32),
            dma((3,)), dma((NCH, 8)), dma((NCH, 8)), dma((NCH,)), dma((NCH,)),
            dma((8, NCH)), dma((8, NCH)), dma((8, NCH)), dma((8, NCH)),
            dma((NCH, 4)), dma((NCH, 4)), dma((7, NCH)), dma((7, NCH)),
            dma((NCH, 8)), dma((NCH, 8)), dma((NCH,)), dma((NCH,)),
        ],
        name="apply_experts",
        compiler_params=pltpu.CompilerParams(
            collective_id=1, has_side_effects=True, vmem_limit_bytes=60 << 20
        ),
    )(*operands)


def rotation(positions):
    steps = np.arange(HD // 2, dtype=np.float32) / np.float32(HD // 2)
    freq = (np.float64(ROPE_BASE) ** -steps.astype(np.float64)).astype(np.float32)
    angles = positions.astype(np.float32)[:, None] * freq[None, :]
    cosine, sine = np.cos(angles.astype(np.float64)), np.sin(angles.astype(np.float64))
    return (
        jnp.asarray(np.concatenate([cosine, cosine], axis=1), F32),
        jnp.asarray(np.concatenate([-sine, sine], axis=1), F32),
    )


def per_device(
    hidden_in, queries, question_kv, passage_kv, use_lists, offsets, out_weight, norm_gain,
    router, routes, w_gate, w_up, w_down,
):
    qcos, qsin = rotation(PUSE * (PLEN + GAP) + np.arange(QTOK))
    starts = np.arange(PUSE)[:, None] * (PLEN + GAP) + np.arange(GAP)[None, :]
    pcos, psin = rotation(starts.reshape(-1))
    resid, packed, gates = attention(
        jnp.concatenate([use_lists, offsets], axis=1), passage_kv, queries, question_kv, qcos, qsin, pcos, psin, out_weight,
        hidden_in, norm_gain.reshape(1, D), router.T, routes.T,
    )
    return experts(packed, gates, resid, w_gate[0], w_up[0], w_down[0])


def solution(mesh):
    in_specs = (
        P(("req", "exp"), None),
        P("req", "exp"),
        P("req", None),
        P("req", "exp", None),
        P(),
        P(),
        P("exp", "req"),
        P(),
        P(),
        P(("req", "exp"), None),
        P("req", None, "exp"),
        P("req", None, "exp"),
        P("req", "exp", None),
    )
    return jax.shard_map(
        per_device, mesh=mesh, in_specs=in_specs, out_specs=P(("req", "exp"), None), check_vma=False
    )
```

```python
import math

import jax
import jax.numpy as jnp
import numpy as np
from jax import lax
from jax.experimental import pallas as pl
from jax.experimental.pallas import tpu as pltpu
from jax.sharding import PartitionSpec as P

D = 6144
HALF = D // 2
HQ = 48
KVH = 8
HD = 128
E = 8
PLEN = 2048
PUSE = 4
PASS_DEV = 4
GAP = 64
C = 5
QTOK = 256
TOK = 16
N_REQ = 8
HID = 512
COLS = D // N_REQ
HEADS = 3
ROPE_BASE = 1000000.0
EPSILON = 1e-05
MESH = pl.DeviceIdType.MESH
F32 = jnp.float32
BF16 = jnp.bfloat16
VMEM = pl.BlockSpec(memory_space=pltpu.VMEM)
SMEM = pl.BlockSpec(memory_space=pltpu.SMEM)
ANY = pl.BlockSpec(memory_space=pl.ANY)
SCALE2 = math.log2(math.e) / math.sqrt(HD)
CHUNKS = (0, 1, 3, 2)
LATE = (0,)
NCH = 3
CW = HALF // NCH
CUT = CW // 2


def place():
    req = lax.axis_index("req")
    exp = lax.axis_index("exp")
    return req, exp, exp // 4, (exp // 2) % 2, exp % 2


def member(z, yh, c):
    return (z * 2 + yh) * 2 + c


def remote(src, dst, send, recv, device):
    return pltpu.make_async_remote_copy(
        src_ref=src, dst_ref=dst, send_sem=send, recv_sem=recv, device_id=device, device_id_type=MESH
    )


def call_out(devices):
    barrier = pltpu.get_barrier_semaphore()
    for device in devices:
        pl.semaphore_signal(barrier, inc=1, device_id=device, device_id_type=MESH)


def greet(devices):
    call_out(devices)
    pl.semaphore_wait(pltpu.get_barrier_semaphore(), len(devices))


def turn(vectors, cosine, sine):
    return vectors * cosine + pltpu.roll(vectors, HD // 2, vectors.ndim - 1) * sine


def loop(count, body):
    lax.fori_loop(0, count, lambda k, carry: (body(k), carry)[1], 0)


def attention_kernel(
    table, pkv, q_h, qkv, qcos_h, qsin_h, pcos_h, psin_h, w_h, attn_out,
    land0, land1, land2, land3, stage, got0, got1, got2, got3,
    kown, ksib, q_in, kvq, qcos, qsin, pcos, psin, qrot, acc, top, low,
    att, w, attb, ownp, sibs, sibr, rss, rsr, fsend, fin,
    ls, s1s, s1r, s2s, s2r, fs, fr,
    a_s, a_r, b_s, b_r, c_s, c_r, d_s, d_r,
):
    req, exp, z, yh, c = place()
    x, yl = req % 4, req // 4
    chip = exp // 2
    mine = req * 2 + yh
    land = (land0, land1, land2, land3)
    got = (got0, got1, got2, got3)
    sibling = (req, member(z, yh, 1 - c))
    chips = [(req, ((chip + d) % 8) * 2 + c) for d in range(1, 8)]
    peers = [((req + d) % N_REQ, exp) for d in range(1, 8)]
    beside = ((1 - yl) * 4 + x, exp)
    right, left = (yl * 4 + (x + 1) % 4, exp), (yl * 4 + (x + 3) % 4, exp)

    loads = [
        pltpu.make_async_copy(src, dst, ls.at[i])
        for i, (src, dst) in enumerate(
            (
                (q_h, q_in),
                (qkv.at[:, pl.ds(pl.multiple_of(chip * 256, 256), 256)], kvq),
                (qcos_h, qcos), (qsin_h, qsin), (pcos_h, pcos), (psin_h, psin),
                (w_h, w),
            )
        )
    ]
    for cp in loads:
        cp.start()

    devices = [(req, member((z + d) % 4, y, c)) for d in range(1, 4) for y in (yh, 1 - yh)]
    devices.append(sibling)
    for k in range(1, 16):
        there = (mine + k) % 16
        devices.append((there // 2, member(z, there % 2, c)))
    greet(devices)

    def cols(zt):
        return pl.ds(pl.multiple_of(zt * 512, 512), 512)

    def first(d):
        zt = (z + d) % 4
        return remote(
            pkv.at[:, :, cols(zt)], land[4 - d], s1s.at[d], s1r.at[4 - d], (req, member(zt, yh, c))
        )

    firsts = {d: first(d) for d in range(1, 4)}
    local = pltpu.make_async_copy(pkv.at[:, :, cols(z)], land0, s1r.at[0])
    local.start()
    firsts[1].start()
    firsts[3].start()

    def half(yt):
        return pl.ds(pl.multiple_of(yt * 256, 256), 256)

    def second(i, k):
        there = (mine + k) % 16
        return remote(
            stage.at[i, there // 2, :, half(there % 2)], got[i].at[mine],
            s2s.at[i, k], s2r.at[i, mine], (there // 2, member(z, there % 2, c)),
        )

    def second_in(i, k):
        there = (mine + k) % 16
        return remote(
            stage.at[i, there // 2, :, half(there % 2)], got[i].at[there],
            s2s.at[i, k], s2r.at[i, there], (there // 2, member(z, there % 2, c)),
        )

    def second_local(i):
        return pltpu.make_async_copy(
            stage.at[i, req, :, half(yh)], got[i].at[mine], s2r.at[i, mine]
        )

    sel = []
    for r in range(N_REQ):
        at = jnp.int32(0)
        for j in range(PUSE):
            p = table[r, j]
            at = at + jnp.where(p // PASS_DEV == req, p % PASS_DEV, 0)
        sel.append(at)
    own = [table[req, j] // PASS_DEV for j in range(PUSE)]
    spot = [
        j * GAP + jnp.clip(table[req, PUSE + j] - j * (PLEN + GAP), 0, GAP - 1) for j in range(PUSE)
    ]

    for i, d in enumerate(CHUNKS):
        if d == 0:
            local.wait()
        else:
            firsts[4 - d].wait_recv()
        for r in range(N_REQ):
            stage[i, r] = land[d][sel[r]]
        loop(15, lambda k: second(i, k + 1).start())
        second_local(i).start()
        if i == 1:
            firsts[2].start()

        if i == 0:
            for cp in loads:
                cp.wait()
            cosine, sine = qcos[...], qsin[...]
            for h in range(HEADS):
                qrot[h * QTOK : (h + 1) * QTOK] = turn(
                    q_in[:, h * HD : (h + 1) * HD].astype(F32), cosine, sine
                ).astype(BF16)
            keys = turn(kvq[:, :HD].astype(F32), cosine, sine).astype(BF16)
            s = lax.dot_general(
                qrot[...], keys, (((1,), (1,)), ((), ())), preferred_element_type=F32
            )
            row = lax.broadcasted_iota(jnp.int32, s.shape, 0) % QTOK
            col = lax.broadcasted_iota(jnp.int32, s.shape, 1)
            s = jnp.where(col <= row, s, -jnp.inf)
            t = jnp.max(s, axis=-1, keepdims=True)
            p = jnp.exp2(s * SCALE2 - t * SCALE2)
            top[...] = jnp.broadcast_to(t, top.shape)
            low[...] = jnp.broadcast_to(jnp.sum(p, axis=-1, keepdims=True), low.shape)
            acc[...] = jnp.dot(p.astype(BF16), kvq[:, HD:], preferred_element_type=F32)

    def attend(block):
        s = lax.dot_general(
            qrot[...], block[:, :HD], (((1,), (1,)), ((), ())), preferred_element_type=F32
        )
        before = top[:, :1]
        t = jnp.maximum(before, jnp.max(s, axis=-1, keepdims=True))
        p = jnp.exp2(s * SCALE2 - t * SCALE2)
        alpha = jnp.exp2((before - t) * SCALE2)
        top[...] = jnp.broadcast_to(t, top.shape)
        low[...] = low[...] * alpha + jnp.sum(p, axis=-1, keepdims=True)
        acc[...] = acc[...] * alpha + jnp.dot(
            p.astype(BF16), block[:, HD:], preferred_element_type=F32
        )

    passes = []
    for i in range(4):
        loop(15, lambda k: second_in(i, k + 1).wait_recv())
        second_local(i).wait()
        for j in range(PUSE):
            cosine, sine = pcos[pl.ds(spot[j], 1), :], psin[pl.ds(spot[j], 1), :]
            for y in range(2):
                kv = got[i][own[j] * 2 + y]
                rows = pl.ds(j * 256 + y * 128, 128)
                kown[i, rows, :HD] = turn(kv[:, :HD].astype(F32), cosine, sine).astype(BF16)
                kown[i, rows, HD:] = kv[:, HD:]
        cp = remote(kown.at[i], ksib.at[i], fs.at[i], fr.at[i], sibling)
        cp.start()
        passes.append(cp)
        attend(kown.at[i])
        cp.wait_recv()
        attend(ksib.at[i])

    for h in range(HEADS):
        rows = pl.ds(h * QTOK, QTOK)
        att[:, :, :, h * HD : (h + 1) * HD] = (
            (acc[rows, :] / low[rows, :]).astype(BF16).reshape(8, 2, TOK, HD)
        )

    def gather(i, src, xr, side, device):
        cp = remote(src, attb.at[xr, side], a_s.at[i], a_r.at[i], device)
        cp.start()
        return cp

    swap = gather(0, att, 0, 1, beside)
    right0 = gather(1, att, 3, 0, right)
    left0 = gather(2, att, 1, 0, left)

    def multiply(k, source):
        theirs = source[:, 1 - c].reshape(128, 384)
        sibs[k] = jnp.dot(theirs, w[...], preferred_element_type=F32).astype(BF16).reshape(8, TOK, COLS)
        cp = remote(sibs.at[k], sibr.at[k], b_s.at[k], b_r.at[k], sibling)
        cp.start()
        ours = source[:, c].reshape(128, 384)
        ownp[k] = jnp.dot(ours, w[...], preferred_element_type=F32).reshape(8, TOK, COLS)
        return cp

    def scatter(k, cp):
        cp.wait_recv()
        rss[k] = (ownp[k] + sibr[k].astype(F32)).astype(BF16)
        rsr[k, chip] = rss[k, chip]
        copies = []
        for d in range(1, 8):
            there = (chip + d) % 8
            cp = remote(rss.at[k, there], rsr.at[k, chip], c_s.at[k, d], c_r.at[k, d], chips[d - 1])
            cp.start()
            copies.append(cp)
        return copies

    order = ((0, 0), (0, 1), (3, 0), (1, 0), (1, 1), (3, 1), (2, 0), (2, 1))

    def finish(k, copies):
        for cp in copies:
            cp.wait_recv()
        total = jnp.sum(rsr[k].astype(F32), axis=0).astype(BF16)
        if k == 0:
            fin[req] = total
            return None
        fsend[k] = total
        xr, side = order[k]
        target = (jnp.abs(yl - side) * 4 + (x + xr) % 4, exp)
        cp = remote(fsend.at[k], fin.at[req], d_s.at[k], d_r.at[k], target)
        cp.start()
        return cp

    halves, parts, ends, gathers = {}, {}, {}, [swap, right0, left0]
    for k in range(8 + 4):
        if k < 8:
            if k == 1:
                swap.wait_recv()
                right1 = gather(3, attb.at[0, 1], 3, 1, right)
                left1 = gather(4, attb.at[0, 1], 1, 1, left)
                right0.wait_recv()
                right2 = gather(5, attb.at[3, 0], 2, 0, right)
                gathers += [right1, left1, right2]
            elif k == 3:
                left0.wait_recv()
            elif k == 4:
                left1.wait_recv()
                left2 = gather(6, attb.at[1, 1], 2, 1, left)
                gathers.append(left2)
            elif k == 5:
                right1.wait_recv()
            elif k == 6:
                right2.wait_recv()
            elif k == 7:
                left2.wait_recv()
            halves[k] = multiply(k, att if k == 0 else attb.at[order[k][0], order[k][1]])
        if 0 <= k - 1 < 8:
            parts[k - 1] = scatter(k - 1, halves[k - 1])
        if 0 <= k - 4 < 8:
            ends[k - 4] = finish(k - 4, parts[k - 4])
    for k in range(1, 8):
        ends[k].wait_recv()

    for i in range(N_REQ):
        attn_out[:, i * COLS : (i + 1) * COLS] = fin[i]

    for cp in list(firsts.values()) + passes + gathers:
        cp.wait_send()
    for i in range(4):
        loop(15, lambda k: second(i, k + 1).wait_send())
    for k in range(8):
        halves[k].wait_send()
        for cp in parts[k]:
            cp.wait_send()
        if k > 0:
            ends[k].wait_send()


def attention(*operands):
    dma = pltpu.SemaphoreType.DMA
    v = pltpu.VMEM
    return pl.pallas_call(
        attention_kernel,
        out_shape=jax.ShapeDtypeStruct((TOK, D), BF16),
        in_specs=[SMEM] + [ANY] * 8,
        out_specs=VMEM,
        scratch_shapes=[v((PASS_DEV, 128, 512), BF16)] * 4
        + [v((4, N_REQ, 128, 512), BF16)]
        + [v((16, 128, 256), BF16)] * 4
        + [
            v((4, 1024, 256), BF16), v((4, 1024, 256), BF16),
            v((QTOK, HEADS * HD), BF16), v((QTOK, 256), BF16),
            v((QTOK, HD), F32), v((QTOK, HD), F32),
            v((PUSE * GAP, HD), F32), v((PUSE * GAP, HD), F32),
            v((HEADS * QTOK, HD), BF16),
            v((HEADS * QTOK, HD), F32), v((HEADS * QTOK, HD), F32), v((HEADS * QTOK, HD), F32),
            v((8, 2, TOK, 384), BF16), v((384, COLS), BF16), v((4, 2, 8, 2, TOK, 384), BF16),
            v((8, 8, TOK, COLS), F32),
            v((8, 8, TOK, COLS), BF16), v((8, 8, TOK, COLS), BF16),
            v((8, 8, TOK, COLS), BF16), v((8, 8, TOK, COLS), BF16),
            v((8, TOK, COLS), BF16), v((8, TOK, COLS), BF16),
            dma((7,)), dma((4,)), dma((4,)), dma((4, 16)), dma((4, 16)), dma((4,)), dma((4,)),
            dma((7,)), dma((7,)), dma((8,)), dma((8,)), dma((8, 8)), dma((8, 8)),
            dma((8,)), dma((8,)),
        ],
        name="attend_and_project",
        compiler_params=pltpu.CompilerParams(
            collective_id=0, has_side_effects=True, vmem_limit_bytes=56 << 20
        ),
    )(*operands)


def expert_kernel(
    attn, routes, hid_h, gain_h, router_h, wg_h, wu_h, wd_h, out,
    hid, gain, router, resid, packed, nsend, nbuf, pbuf, gates,
    wg, wu, wd, prx, xo, xs, gu, inner, po, sps, spr, rzs, rz, ysend, ry, kept, bsend, ret,
    mixed, mrecv,
    w_s, e_s, e_r, a_s, a_r, y_s, y_r, g_s, g_r, f_s, f_r, p_s, p_r, r_s, r_r, t_s, t_r, m_s, m_r,
):
    req, exp, z, yh, c = place()
    other = 1 - yh
    sibling = (req, member(z, yh, 1 - c))
    across = (req, member(z, other, c))
    up = (req, member((z + 1) % 4, yh, c))
    down = (req, member((z + 3) % 4, yh, c))
    peers = [((req + d) % N_REQ, exp) for d in range(1, 8)]
    loads = [
        pltpu.make_async_copy(src, dst, w_s.at[i])
        for i, (src, dst) in enumerate(
            ((wg_h, wg), (wu_h, wu), (wd_h, wd), (hid_h, hid), (gain_h, gain), (router_h, router))
        )
    ]
    for cp in loads[3:] + loads[:3]:
        cp.start()
    friends = peers + [sibling, across, up, down]
    call_out(friends)

    for cp in loads[3:]:
        cp.wait()
    stream = hid[...].astype(F32) + attn[...].astype(F32)
    resid[...] = stream
    mean = jnp.mean(stream * stream, axis=-1, keepdims=True)
    normed = (stream * lax.rsqrt(mean + EPSILON) * gain[...]).astype(BF16)
    left_half, right_half = normed[:, :HALF], normed[:, HALF:]
    nsend[...] = jnp.where(c == 0, right_half, left_half)
    nbuf[c] = jnp.where(c == 0, left_half, right_half)

    row = lax.broadcasted_iota(jnp.int32, (TOK, TOK), 0)
    col = lax.broadcasted_iota(jnp.int32, (TOK, TOK), 1)
    named = lax.broadcasted_iota(jnp.int32, (TOK, E), 1)
    places = lax.broadcasted_iota(jnp.int32, (TOK, 128), 1)
    choice, hits = [], []
    for k in range(2):
        expert = jnp.sum(jnp.where(row == col, routes[k : k + 1, :], 0), axis=1, keepdims=True)
        choice.append(expert)
        hits.append((named == expert).astype(F32))
    earlier = jnp.dot(
        (col < row).astype(BF16), (hits[0] + hits[1]).astype(BF16), preferred_element_type=F32
    )
    matches = []
    for k in range(2):
        rank = jnp.sum(hits[k] * earlier, axis=1, keepdims=True).astype(jnp.int32)
        matches.append((places == choice[k] * TOK + c * C + rank).astype(F32))
    pbuf[c] = (matches[0] + matches[1]).astype(BF16)
    logits = lax.dot_general(
        normed, router[...], (((1,), (1,)), ((), ())), preferred_element_type=F32
    )
    apart = jnp.sum(logits * (hits[0] - hits[1]), axis=-1, keepdims=True)
    shares_of = matches[0] * jax.nn.sigmoid(apart) + matches[1] * jax.nn.sigmoid(-apart)
    coarse = shares_of.astype(BF16)
    gates[c, 0] = coarse
    gates[c, 1] = (shares_of - coarse.astype(F32)).astype(BF16)
    pl.semaphore_wait(pltpu.get_barrier_semaphore(), len(friends))

    started = []

    def go(cp):
        cp.start()
        started.append(cp)
        return cp

    lasts = [
        go(remote(nsend, nbuf.at[c], e_s.at[0], e_r.at[0], sibling)),
        go(remote(pbuf.at[c], pbuf.at[c], e_s.at[1], e_r.at[1], sibling)),
        go(remote(gates.at[c], gates.at[c], e_s.at[2], e_r.at[2], sibling)),
    ]
    lasts[0].wait_recv()
    lasts[1].wait_recv()
    packed[...] = (
        lax.dot_general(
            pbuf[...].reshape(32, 128), nbuf[...].reshape(32, HALF), (((0,), (0,)), ((), ())),
            preferred_element_type=F32,
        )
        .astype(BF16)
        .reshape(E, TOK, HALF)
    )

    def part(i):
        return pl.ds(i * CW, CW)

    row = lax.broadcasted_iota(jnp.int32, (80, 128), 0)
    col = lax.broadcasted_iota(jnp.int32, (80, 128), 1)
    pick = (col == row // 10 * TOK + row % 10).astype(BF16)
    row = lax.broadcasted_iota(jnp.int32, (128, 80), 1)
    col = lax.broadcasted_iota(jnp.int32, (128, 80), 0)
    spread = (col == row // 10 * TOK + row % 10).astype(BF16)

    arrive = []
    for i in range(NCH):
        copies = []
        for d in range(1, 8):
            there = (req + d) % N_REQ
            copies.append(
                go(remote(
                    packed.at[there, :, part(i)], prx.at[i, req], a_s.at[i, d], a_r.at[i, d], peers[d - 1]
                ))
            )
        prx[i, req] = packed[req, :, i * CW : (i + 1) * CW]
        arrive.append(copies)

    def ring(n, i, src_at, dst_at, device):
        return go(remote(
            xo.at[(i,) + src_at], xo.at[(i,) + dst_at], g_s.at[n, i], g_r.at[n, i], device
        ))

    shares = {}

    def share(i, zr, y, second):
        at = zr * 2 + second
        shares[i, zr, second] = go(remote(
            xo.at[i, zr, y], xs.at[i, zr, y], f_s.at[at, i], f_r.at[at, i], sibling
        ))

    swap, up1, down1, up2, down2, up3, down3 = {}, {}, {}, {}, {}, {}, {}
    over1, over2, over3 = {}, {}, {}
    lower, upper = (slice(None), pl.ds(0, CUT)), (slice(None), pl.ds(CUT, CUT))
    for i in range(NCH):
        for cp in arrive[i]:
            cp.wait_recv()
        xo[i, 0, yh] = jnp.dot(
            pick, prx[i].reshape(128, CW), preferred_element_type=F32
        ).astype(BF16)
        swap[i] = ring(0, i, (0, yh), (0, yh), across)
        up1[i] = ring(1, i, (0, yh), (3, yh), up)
        down1[i] = ring(2, i, (0, yh), (1, yh), down)
        share(i, 0, yh, 0)
    for i in range(NCH):
        if i in LATE:
            up1[i].wait_recv()
            up3[i] = ring(5, i, (3, yh) + lower, (2, yh) + lower, up)
            over3[i] = ring(3, i, (3, yh), (3, yh), across)
            share(i, 3, yh, 0)
            down1[i].wait_recv()
            down3[i] = ring(6, i, (1, yh) + upper, (2, yh) + upper, down)
            over1[i] = ring(4, i, (1, yh), (1, yh), across)
            share(i, 1, yh, 0)
            swap[i].wait_recv()
            share(i, 0, other, 1)
        else:
            swap[i].wait_recv()
            up2[i] = ring(3, i, (0, other), (3, other), up)
            down2[i] = ring(4, i, (0, other), (1, other), down)
            share(i, 0, other, 1)
            up1[i].wait_recv()
            up3[i] = ring(5, i, (3, yh), (2, yh), up)
            share(i, 3, yh, 0)
            down1[i].wait_recv()
            share(i, 1, yh, 0)

    def hidden(i, zr):
        shares[i, zr, 0].wait_recv()
        shares[i, zr, 1].wait_recv()
        near = pl.ds(pl.multiple_of(c * HALF + i * CW, CW), CW)
        far = pl.ds(pl.multiple_of((1 - c) * HALF + i * CW, CW), CW)
        a, b = xo[i, zr].reshape(160, CW), xs[i, zr].reshape(160, CW)
        for n, weights in enumerate((wg, wu)):
            value = jnp.dot(a, weights[near, :], preferred_element_type=F32)
            value = value + jnp.dot(b, weights[far, :], preferred_element_type=F32)
            if i > 0:
                value = value + gu[zr, n]
            gu[zr, n] = value

    sums = {}

    def result(zr):
        inner[...] = (jax.nn.silu(gu[zr, 0]) * gu[zr, 1]).astype(BF16)
        for i in range(NCH):
            near = pl.ds(pl.multiple_of(c * HALF + i * CW, CW), CW)
            far = pl.ds(pl.multiple_of((1 - c) * HALF + i * CW, CW), CW)
            sps[i, zr] = (
                jnp.dot(inner[...], wd[:, far], preferred_element_type=F32)
                .astype(BF16)
                .reshape(2, 80, CW)
            )
            sums[i, zr] = go(remote(
                sps.at[i, zr], spr.at[i, zr], p_s.at[i, zr], p_r.at[i, zr], sibling
            ))
            po[i, zr] = (
                jnp.dot(inner[...], wd[:, near], preferred_element_type=F32)
                .astype(BF16)
                .reshape(2, 80, CW)
            )

    def total(i, zr, y):
        return po[i, zr, y].astype(F32) + spr[i, zr, y].astype(F32)

    def pass_on(n, i, value, device):
        rzs[n, i] = value.astype(BF16)
        return go(remote(rzs.at[n, i], rz.at[n, i], r_s.at[n, i], r_r.at[n, i], device))

    loads[0].wait()
    loads[1].wait()
    for i in range(NCH):
        hidden(i, 0)
    for i in range(NCH):
        if i in LATE:
            up3[i].wait_recv()
            down3[i].wait_recv()
            over2[i] = ring(7, i, (2, yh), (2, yh), across)
            share(i, 2, yh, 0)
            over1[i].wait_recv()
            share(i, 1, other, 1)
            over3[i].wait_recv()
            share(i, 3, other, 1)
        else:
            down2[i].wait_recv()
            down3[i] = ring(6, i, (1, other), (2, other), down)
            share(i, 1, other, 1)
            up2[i].wait_recv()
            share(i, 3, other, 1)
        hidden(i, 1)
        hidden(i, 3)
    loads[2].wait()
    result(1)
    result(3)
    early = [i for i in range(NCH) if i not in LATE]
    to_up, to_down, far_up, far_down, near_up, near_down = {}, {}, {}, {}, {}, {}
    cross, cross1, cross2, cross3, back = {}, {}, {}, {}, {}
    for i in range(NCH):
        sums[i, 1].wait_recv()
        sums[i, 3].wait_recv()
        if i in LATE:
            cross1[i] = pass_on(0, i, total(i, 1, other), across)
            cross3[i] = pass_on(1, i, total(i, 3, other), across)
        else:
            to_up[i] = pass_on(0, i, total(i, 1, other), up)
            to_down[i] = pass_on(1, i, total(i, 3, yh), down)
    for i in range(NCH):
        if i in LATE:
            over2[i].wait_recv()
            share(i, 2, other, 1)
        else:
            up3[i].wait_recv()
            share(i, 2, yh, 0)
            down3[i].wait_recv()
            share(i, 2, other, 1)
        if i > 0:
            hidden(i - 1, 2)
    hidden(NCH - 1, 2)
    result(2)
    for i in range(NCH):
        sums[i, 2].wait_recv()
        if i in LATE:
            cross2[i] = pass_on(6, i, total(i, 2, other), across)
        else:
            far_up[i] = pass_on(2, i, total(i, 2, yh), up)
            far_down[i] = pass_on(3, i, total(i, 2, other), down)
    result(0)

    def cross_over(i, value):
        ysend[i] = value.astype(BF16)
        cross[i] = go(remote(ysend.at[i], ry.at[i], y_s.at[i], y_r.at[i], across))

    for i in LATE:
        sums[i, 0].wait_recv()
        cross_over(i, total(i, 0, other))
        cross2[i].wait_recv()
        both = (total(i, 2, yh) + rz[6, i].astype(F32)).astype(BF16)
        rzs[2, i, :, :CUT] = both[:, :CUT]
        rzs[3, i, :, CUT:] = both[:, CUT:]
        for n, cols, device, copies in ((2, lower, up, far_up), (3, upper, down, far_down)):
            copies[i] = go(remote(
                rzs.at[(n, i) + cols], rz.at[(n, i) + cols], r_s.at[n, i], r_r.at[n, i], device
            ))
    for i in early:
        far_up[i].wait_recv()
        near_up[i] = pass_on(4, i, total(i, 1, yh) + rz[2, i].astype(F32), up)
        far_down[i].wait_recv()
        near_down[i] = pass_on(5, i, total(i, 3, other) + rz[3, i].astype(F32), down)
    for i in LATE:
        cross1[i].wait_recv()
        cross3[i].wait_recv()
        far_up[i].wait_recv()
        far_down[i].wait_recv()
        ahead = total(i, 1, yh) + rz[0, i].astype(F32)
        behind = total(i, 3, yh) + rz[1, i].astype(F32)
        added = jnp.concatenate(
            [ahead[:, :CUT] + rz[2, i, :, :CUT].astype(F32), ahead[:, CUT:]], axis=1
        )
        near_up[i] = pass_on(4, i, added, up)
        added = jnp.concatenate(
            [behind[:, :CUT], behind[:, CUT:] + rz[3, i, :, CUT:].astype(F32)], axis=1
        )
        near_down[i] = pass_on(5, i, added, down)

    def gathered(i):
        sums[i, 0].wait_recv()
        to_up[i].wait_recv()
        near_down[i].wait_recv()
        cross_over(i, total(i, 0, other) + rz[0, i].astype(F32) + rz[5, i].astype(F32))
        to_down[i].wait_recv()
        near_up[i].wait_recv()
        kept[i] = total(i, 0, yh) + rz[1, i].astype(F32) + rz[4, i].astype(F32)

    def give_back(i):
        cross[i].wait_recv()
        done = kept[i] + ry[i].astype(F32)
        if i in LATE:
            near_up[i].wait_recv()
            near_down[i].wait_recv()
            done = done + rz[4, i].astype(F32) + rz[5, i].astype(F32)
        bsend[i] = (
            jnp.dot(spread, done.astype(BF16), preferred_element_type=F32)
            .astype(BF16)
            .reshape(N_REQ, TOK, CW)
        )
        copies = []
        for d in range(1, 8):
            there = (req + d) % N_REQ
            copies.append(go(remote(
                bsend.at[i, there], ret.at[i, req], t_s.at[i, d], t_r.at[i, d], peers[d - 1]
            )))
        ret[i, req] = bsend[i, req]
        back[i] = copies

    for i in LATE:
        kept[i] = total(i, 0, yh)
    gathered(early[0])
    for n in range(1, len(early)):
        gathered(early[n])
        give_back(early[n - 1])
    give_back(early[-1])
    for i in LATE:
        give_back(i)
    mix = {}
    lasts[2].wait_recv()
    for i in early + list(LATE):
        for cp in back[i]:
            cp.wait_recv()
        terms = jnp.dot(
            gates[...].reshape(4 * TOK, 128), ret[i].reshape(128, CW), preferred_element_type=F32
        ).reshape(2, 2, TOK, CW)
        mixed[i] = terms[:, 0] + terms[:, 1]
        mix[i] = go(remote(mixed.at[i, 1 - c], mrecv.at[i], m_s.at[i], m_r.at[i], sibling))
        near = pl.ds(pl.multiple_of(c * HALF + i * CW, CW), CW)
        out[:, near] = (resid[:, near] + mixed[i, c]).astype(BF16)
    for i in early + list(LATE):
        mix[i].wait_recv()
        far = pl.ds(pl.multiple_of((1 - c) * HALF + i * CW, CW), CW)
        out[:, far] = (resid[:, far] + mrecv[i]).astype(BF16)
    for cp in started:
        cp.wait_send()


def experts(*operands):
    dma = pltpu.SemaphoreType.DMA
    v = pltpu.VMEM
    return pl.pallas_call(
        expert_kernel,
        out_shape=jax.ShapeDtypeStruct((TOK, D), BF16),
        in_specs=[VMEM] * 2 + [ANY] * 6,
        out_specs=VMEM,
        scratch_shapes=[
            v((TOK, D), BF16), v((1, D), F32), v((E, D), BF16), v((TOK, D), F32),
            v((E, TOK, HALF), BF16), v((TOK, HALF), BF16), v((2, TOK, HALF), BF16),
            v((2, TOK, 128), BF16), v((2, 2, TOK, 128), BF16),
            v((D, HID), BF16), v((D, HID), BF16), v((HID, D), BF16),
            v((NCH, N_REQ, TOK, CW), BF16),
            v((NCH, 4, 2, 80, CW), BF16), v((NCH, 4, 2, 80, CW), BF16),
            v((4, 2, 160, HID), F32),
            v((160, HID), BF16),
            v((NCH, 4, 2, 80, CW), BF16), v((NCH, 4, 2, 80, CW), BF16), v((NCH, 4, 2, 80, CW), BF16),
            v((7, NCH, 80, CW), BF16), v((7, NCH, 80, CW), BF16),
            v((NCH, 80, CW), BF16), v((NCH, 80, CW), BF16), v((NCH, 80, CW), F32),
            v((NCH, N_REQ, TOK, CW), BF16), v((NCH, N_REQ, TOK, CW), BF16),
            v((NCH, 2, TOK, CW), F32), v((NCH, TOK, CW), F32),
            dma((6,)), dma((3,)), dma((3,)), dma((NCH, 8)), dma((NCH, 8)), dma((NCH,)), dma((NCH,)),
            dma((8, NCH)), dma((8, NCH)), dma((8, NCH)), dma((8, NCH)),
            dma((NCH, 4)), dma((NCH, 4)), dma((7, NCH)), dma((7, NCH)),
            dma((NCH, 8)), dma((NCH, 8)), dma((NCH,)), dma((NCH,)),
        ],
        name="apply_experts",
        compiler_params=pltpu.CompilerParams(
            collective_id=1, has_side_effects=True, vmem_limit_bytes=60 << 20
        ),
    )(*operands)


def rotation(positions):
    steps = np.arange(HD // 2, dtype=np.float32) / np.float32(HD // 2)
    freq = (np.float64(ROPE_BASE) ** -steps.astype(np.float64)).astype(np.float32)
    angles = positions.astype(np.float32)[:, None] * freq[None, :]
    cosine, sine = np.cos(angles.astype(np.float64)), np.sin(angles.astype(np.float64))
    return (
        jnp.asarray(np.concatenate([cosine, cosine], axis=1), F32),
        jnp.asarray(np.concatenate([-sine, sine], axis=1), F32),
    )


def per_device(
    hidden_in, queries, question_kv, passage_kv, use_lists, offsets, out_weight, norm_gain,
    router, routes, w_gate, w_up, w_down,
):
    qcos, qsin = rotation(PUSE * (PLEN + GAP) + np.arange(QTOK))
    starts = np.arange(PUSE)[:, None] * (PLEN + GAP) + np.arange(GAP)[None, :]
    pcos, psin = rotation(starts.reshape(-1))
    attn = attention(
        jnp.concatenate([use_lists, offsets], axis=1), passage_kv, queries, question_kv,
        qcos, qsin, pcos, psin, out_weight,
    )
    return experts(
        attn, routes.T, hidden_in, norm_gain.reshape(1, D), router.T, w_gate[0], w_up[0], w_down[0]
    )


def solution(mesh):
    in_specs = (
        P(("req", "exp"), None),
        P("req", "exp"),
        P("req", None),
        P("req", "exp", None),
        P(),
        P(),
        P("exp", "req"),
        P(),
        P(),
        P(("req", "exp"), None),
        P("req", None, "exp"),
        P("req", None, "exp"),
        P("req", "exp", None),
    )
    return jax.shard_map(
        per_device, mesh=mesh, in_specs=in_specs, out_specs=P(("req", "exp"), None), check_vma=False
    )
```

```python
import math

import jax
import jax.numpy as jnp
import numpy as np
from jax import lax
from jax.experimental import pallas as pl
from jax.experimental.pallas import tpu as pltpu
from jax.sharding import PartitionSpec as P

D = 6144
HALF = D // 2
HQ = 48
KVH = 8
HD = 128
E = 8
PLEN = 2048
PUSE = 4
PASS_DEV = 4
GAP = 64
C = 5
QTOK = 256
TOK = 16
N_REQ = 8
HID = 512
COLS = D // N_REQ
HEADS = 3
ROPE_BASE = 1000000.0
EPSILON = 1e-05
MESH = pl.DeviceIdType.MESH
F32 = jnp.float32
BF16 = jnp.bfloat16
VMEM = pl.BlockSpec(memory_space=pltpu.VMEM)
SMEM = pl.BlockSpec(memory_space=pltpu.SMEM)
ANY = pl.BlockSpec(memory_space=pl.ANY)
SCALE2 = math.log2(math.e) / math.sqrt(HD)
CHUNKS = (0, 1, 3, 2)
LATE = (0,)
NCH = 3
CW = HALF // NCH
CUT = CW // 2


def place():
    req = lax.axis_index("req")
    exp = lax.axis_index("exp")
    return req, exp, exp // 4, (exp // 2) % 2, exp % 2


def member(z, yh, c):
    return (z * 2 + yh) * 2 + c


def remote(src, dst, send, recv, device):
    return pltpu.make_async_remote_copy(
        src_ref=src, dst_ref=dst, send_sem=send, recv_sem=recv, device_id=device, device_id_type=MESH
    )


def call_out(devices):
    barrier = pltpu.get_barrier_semaphore()
    for device in devices:
        pl.semaphore_signal(barrier, inc=1, device_id=device, device_id_type=MESH)


def greet(devices):
    call_out(devices)
    pl.semaphore_wait(pltpu.get_barrier_semaphore(), len(devices))


def turn(vectors, cosine, sine):
    return vectors * cosine + pltpu.roll(vectors, HD // 2, vectors.ndim - 1) * sine


def loop(count, body):
    lax.fori_loop(0, count, lambda k, carry: (body(k), carry)[1], 0)


def attention_kernel(
    table, pkv, q_h, qkv, qcos_h, qsin_h, pcos_h, psin_h, w_h, attn_out,
    land0, land1, land2, land3, stage, got0, got1, got2, got3,
    kown, ksib, q_in, kvq, qcos, qsin, pcos, psin, qrot, acc, top, low,
    att, w, attb, ownp, sibs, sibr, rss, rsr, fsend, fin,
    ls, s1s, s1r, s2s, s2r, fs, fr,
    a_s, a_r, b_s, b_r, c_s, c_r, d_s, d_r,
):
    req, exp, z, yh, c = place()
    x, yl = req % 4, req // 4
    chip = exp // 2
    mine = req * 2 + yh
    land = (land0, land1, land2, land3)
    got = (got0, got1, got2, got3)
    sibling = (req, member(z, yh, 1 - c))
    chips = [(req, ((chip + d) % 8) * 2 + c) for d in range(1, 8)]
    peers = [((req + d) % N_REQ, exp) for d in range(1, 8)]
    beside = ((1 - yl) * 4 + x, exp)
    right, left = (yl * 4 + (x + 1) % 4, exp), (yl * 4 + (x + 3) % 4, exp)

    loads = [
        pltpu.make_async_copy(src, dst, ls.at[i])
        for i, (src, dst) in enumerate(
            (
                (q_h, q_in),
                (qkv.at[:, pl.ds(pl.multiple_of(chip * 256, 256), 256)], kvq),
                (qcos_h, qcos), (qsin_h, qsin), (pcos_h, pcos), (psin_h, psin),
                (w_h, w),
            )
        )
    ]
    for cp in loads:
        cp.start()

    devices = [(req, member((z + d) % 4, y, c)) for d in range(1, 4) for y in (yh, 1 - yh)]
    devices.append(sibling)
    for k in range(1, 16):
        there = (mine + k) % 16
        devices.append((there // 2, member(z, there % 2, c)))
    greet(devices)

    def cols(zt):
        return pl.ds(pl.multiple_of(zt * 512, 512), 512)

    def first(d):
        zt = (z + d) % 4
        return remote(
            pkv.at[:, :, cols(zt)], land[4 - d], s1s.at[d], s1r.at[4 - d], (req, member(zt, yh, c))
        )

    firsts = {d: first(d) for d in range(1, 4)}
    local = pltpu.make_async_copy(pkv.at[:, :, cols(z)], land0, s1r.at[0])
    local.start()
    firsts[1].start()
    firsts[3].start()

    def half(yt):
        return pl.ds(pl.multiple_of(yt * 256, 256), 256)

    def second(i, k):
        there = (mine + k) % 16
        return remote(
            stage.at[i, there // 2, :, half(there % 2)], got[i].at[mine],
            s2s.at[i, k], s2r.at[i, mine], (there // 2, member(z, there % 2, c)),
        )

    def second_in(i, k):
        there = (mine + k) % 16
        return remote(
            stage.at[i, there // 2, :, half(there % 2)], got[i].at[there],
            s2s.at[i, k], s2r.at[i, there], (there // 2, member(z, there % 2, c)),
        )

    def second_local(i):
        return pltpu.make_async_copy(
            stage.at[i, req, :, half(yh)], got[i].at[mine], s2r.at[i, mine]
        )

    sel = []
    for r in range(N_REQ):
        at = jnp.int32(0)
        for j in range(PUSE):
            p = table[j, r]
            at = at + jnp.where(p // PASS_DEV == req, p % PASS_DEV, 0)
        sel.append(at)
    own = [table[j, req] // PASS_DEV for j in range(PUSE)]
    spot = [
        j * GAP + jnp.clip(table[PUSE + j, req] - j * (PLEN + GAP), 0, GAP - 1) for j in range(PUSE)
    ]

    for i, d in enumerate(CHUNKS):
        if d == 0:
            local.wait()
        else:
            firsts[4 - d].wait_recv()
        for r in range(N_REQ):
            stage[i, r] = land[d][sel[r]]
        loop(15, lambda k: second(i, k + 1).start())
        second_local(i).start()
        if i == 1:
            firsts[2].start()

        if i == 0:
            for cp in loads:
                cp.wait()
            cosine, sine = qcos[...], qsin[...]
            for h in range(HEADS):
                qrot[h * QTOK : (h + 1) * QTOK] = turn(
                    q_in[:, h * HD : (h + 1) * HD].astype(F32), cosine, sine
                ).astype(BF16)
            keys = turn(kvq[:, :HD].astype(F32), cosine, sine).astype(BF16)
            s = lax.dot_general(
                qrot[...], keys, (((1,), (1,)), ((), ())), preferred_element_type=F32
            )
            row = lax.broadcasted_iota(jnp.int32, s.shape, 0) % QTOK
            col = lax.broadcasted_iota(jnp.int32, s.shape, 1)
            s = jnp.where(col <= row, s, -jnp.inf)
            t = jnp.max(s, axis=-1, keepdims=True)
            p = jnp.exp2(s * SCALE2 - t * SCALE2)
            top[...] = jnp.broadcast_to(t, top.shape)
            low[...] = jnp.broadcast_to(jnp.sum(p, axis=-1, keepdims=True), low.shape)
            acc[...] = jnp.dot(p.astype(BF16), kvq[:, HD:], preferred_element_type=F32)

    def attend(block):
        s = lax.dot_general(
            qrot[...], block[:, :HD], (((1,), (1,)), ((), ())), preferred_element_type=F32
        )
        before = top[:, :1]
        t = jnp.maximum(before, jnp.max(s, axis=-1, keepdims=True))
        p = jnp.exp2(s * SCALE2 - t * SCALE2)
        alpha = jnp.exp2((before - t) * SCALE2)
        top[...] = jnp.broadcast_to(t, top.shape)
        low[...] = low[...] * alpha + jnp.sum(p, axis=-1, keepdims=True)
        acc[...] = acc[...] * alpha + jnp.dot(
            p.astype(BF16), block[:, HD:], preferred_element_type=F32
        )

    passes = []
    for i in range(4):
        loop(15, lambda k: second_in(i, k + 1).wait_recv())
        second_local(i).wait()
        for j in range(PUSE):
            cosine, sine = pcos[pl.ds(spot[j], 1), :], psin[pl.ds(spot[j], 1), :]
            for y in range(2):
                kv = got[i][own[j] * 2 + y]
                rows = pl.ds(j * 256 + y * 128, 128)
                kown[i, rows, :HD] = turn(kv[:, :HD].astype(F32), cosine, sine).astype(BF16)
                kown[i, rows, HD:] = kv[:, HD:]
        cp = remote(kown.at[i], ksib.at[i], fs.at[i], fr.at[i], sibling)
        cp.start()
        passes.append(cp)
        attend(kown.at[i])
        cp.wait_recv()
        attend(ksib.at[i])

    for h in range(HEADS):
        rows = pl.ds(h * QTOK, QTOK)
        att[:, :, :, h * HD : (h + 1) * HD] = (
            (acc[rows, :] / low[rows, :]).astype(BF16).reshape(8, 2, TOK, HD)
        )

    def gather(i, src, xr, side, device):
        cp = remote(src, attb.at[xr, side], a_s.at[i], a_r.at[i], device)
        cp.start()
        return cp

    swap = gather(0, att, 0, 1, beside)
    right0 = gather(1, att, 3, 0, right)
    left0 = gather(2, att, 1, 0, left)

    def multiply(k, source):
        theirs = source[:, 1 - c].reshape(128, 384)
        sibs[k] = jnp.dot(theirs, w[...], preferred_element_type=F32).astype(BF16).reshape(8, TOK, COLS)
        cp = remote(sibs.at[k], sibr.at[k], b_s.at[k], b_r.at[k], sibling)
        cp.start()
        ours = source[:, c].reshape(128, 384)
        ownp[k] = jnp.dot(ours, w[...], preferred_element_type=F32).reshape(8, TOK, COLS)
        return cp

    def scatter(k, cp):
        cp.wait_recv()
        rss[k] = (ownp[k] + sibr[k].astype(F32)).astype(BF16)
        rsr[k, chip] = rss[k, chip]
        copies = []
        for d in range(1, 8):
            there = (chip + d) % 8
            cp = remote(rss.at[k, there], rsr.at[k, chip], c_s.at[k, d], c_r.at[k, d], chips[d - 1])
            cp.start()
            copies.append(cp)
        return copies

    order = ((0, 0), (0, 1), (3, 0), (1, 0), (1, 1), (3, 1), (2, 0), (2, 1))

    def finish(k, copies):
        for cp in copies:
            cp.wait_recv()
        total = jnp.sum(rsr[k].astype(F32), axis=0).astype(BF16)
        if k == 0:
            fin[req] = total
            return None
        fsend[k] = total
        xr, side = order[k]
        target = (jnp.abs(yl - side) * 4 + (x + xr) % 4, exp)
        cp = remote(fsend.at[k], fin.at[req], d_s.at[k], d_r.at[k], target)
        cp.start()
        return cp

    halves, parts, ends, gathers = {}, {}, {}, [swap, right0, left0]
    for k in range(8 + 3):
        if k < 8:
            if k == 1:
                swap.wait_recv()
                right1 = gather(3, attb.at[0, 1], 3, 1, right)
                left1 = gather(4, attb.at[0, 1], 1, 1, left)
                right0.wait_recv()
                right2 = gather(5, attb.at[3, 0], 2, 0, right)
                gathers += [right1, left1, right2]
            elif k == 3:
                left0.wait_recv()
            elif k == 4:
                left1.wait_recv()
                left2 = gather(6, attb.at[1, 1], 2, 1, left)
                gathers.append(left2)
            elif k == 5:
                right1.wait_recv()
            elif k == 6:
                right2.wait_recv()
            elif k == 7:
                left2.wait_recv()
            halves[k] = multiply(k, att if k == 0 else attb.at[order[k][0], order[k][1]])
        if 0 <= k - 1 < 8:
            parts[k - 1] = scatter(k - 1, halves[k - 1])
        if 0 <= k - 3 < 8:
            ends[k - 3] = finish(k - 3, parts[k - 3])
    for k in range(1, 8):
        ends[k].wait_recv()

    for i in range(N_REQ):
        attn_out[:, i * COLS : (i + 1) * COLS] = fin[i]

    for cp in list(firsts.values()) + passes + gathers:
        cp.wait_send()
    for i in range(4):
        loop(15, lambda k: second(i, k + 1).wait_send())
    for k in range(8):
        halves[k].wait_send()
        for cp in parts[k]:
            cp.wait_send()
        if k > 0:
            ends[k].wait_send()


def attention(*operands):
    dma = pltpu.SemaphoreType.DMA
    v = pltpu.VMEM
    return pl.pallas_call(
        attention_kernel,
        out_shape=jax.ShapeDtypeStruct((TOK, D), BF16),
        in_specs=[SMEM] + [ANY] * 8,
        out_specs=VMEM,
        scratch_shapes=[v((PASS_DEV, 128, 512), BF16)] * 4
        + [v((4, N_REQ, 128, 512), BF16)]
        + [v((16, 128, 256), BF16)] * 4
        + [
            v((4, 1024, 256), BF16), v((4, 1024, 256), BF16),
            v((QTOK, HEADS * HD), BF16), v((QTOK, 256), BF16),
            v((QTOK, HD), F32), v((QTOK, HD), F32),
            v((PUSE * GAP, HD), F32), v((PUSE * GAP, HD), F32),
            v((HEADS * QTOK, HD), BF16),
            v((HEADS * QTOK, HD), F32), v((HEADS * QTOK, HD), F32), v((HEADS * QTOK, HD), F32),
            v((8, 2, TOK, 384), BF16), v((384, COLS), BF16), v((4, 2, 8, 2, TOK, 384), BF16),
            v((8, 8, TOK, COLS), F32),
            v((8, 8, TOK, COLS), BF16), v((8, 8, TOK, COLS), BF16),
            v((8, 8, TOK, COLS), BF16), v((8, 8, TOK, COLS), BF16),
            v((8, TOK, COLS), BF16), v((8, TOK, COLS), BF16),
            dma((7,)), dma((4,)), dma((4,)), dma((4, 16)), dma((4, 16)), dma((4,)), dma((4,)),
            dma((7,)), dma((7,)), dma((8,)), dma((8,)), dma((8, 8)), dma((8, 8)),
            dma((8,)), dma((8,)),
        ],
        name="attend_and_project",
        compiler_params=pltpu.CompilerParams(
            collective_id=0, has_side_effects=True, vmem_limit_bytes=56 << 20
        ),
    )(*operands)


def expert_kernel(
    attn, routes, hid_h, gain_h, router_h, wg_h, wu_h, wd_h, out,
    hid, gain, router, resid, packed, nsend, nbuf, pbuf, gates,
    wg, wu, wd, prx, xo, xs, gu, inner, po, sps, spr, rzs, rz, ysend, ry, kept, bsend, ret,
    mixed, mrecv,
    w_s, e_s, e_r, a_s, a_r, y_s, y_r, g_s, g_r, f_s, f_r, p_s, p_r, r_s, r_r, t_s, t_r, m_s, m_r,
):
    req, exp, z, yh, c = place()
    other = 1 - yh
    sibling = (req, member(z, yh, 1 - c))
    across = (req, member(z, other, c))
    up = (req, member((z + 1) % 4, yh, c))
    down = (req, member((z + 3) % 4, yh, c))
    peers = [((req + d) % N_REQ, exp) for d in range(1, 8)]
    loads = [
        pltpu.make_async_copy(src, dst, w_s.at[i])
        for i, (src, dst) in enumerate(
            ((wg_h, wg), (wu_h, wu), (wd_h, wd), (hid_h, hid), (gain_h, gain), (router_h, router))
        )
    ]
    for cp in loads[3:] + loads[:3]:
        cp.start()
    friends = peers + [sibling, across, up, down]
    call_out(friends)

    for cp in loads[3:]:
        cp.wait()
    stream = hid[...].astype(F32) + attn[...].astype(F32)
    resid[...] = stream
    mean = jnp.mean(stream * stream, axis=-1, keepdims=True)
    normed = (stream * lax.rsqrt(mean + EPSILON) * gain[...]).astype(BF16)
    left_half, right_half = normed[:, :HALF], normed[:, HALF:]
    nsend[...] = jnp.where(c == 0, right_half, left_half)
    nbuf[c] = jnp.where(c == 0, left_half, right_half)

    row = lax.broadcasted_iota(jnp.int32, (TOK, TOK), 0)
    col = lax.broadcasted_iota(jnp.int32, (TOK, TOK), 1)
    named = lax.broadcasted_iota(jnp.int32, (TOK, E), 1)
    places = lax.broadcasted_iota(jnp.int32, (TOK, 128), 1)
    choice, hits = [], []
    for k in range(2):
        expert = jnp.sum(jnp.where(row == col, routes[k : k + 1, :], 0), axis=1, keepdims=True)
        choice.append(expert)
        hits.append((named == expert).astype(F32))
    earlier = jnp.dot(
        (col < row).astype(BF16), (hits[0] + hits[1]).astype(BF16), preferred_element_type=F32
    )
    matches = []
    for k in range(2):
        rank = jnp.sum(hits[k] * earlier, axis=1, keepdims=True).astype(jnp.int32)
        matches.append((places == choice[k] * TOK + c * C + rank).astype(F32))
    pbuf[c] = (matches[0] + matches[1]).astype(BF16)
    logits = lax.dot_general(
        normed, router[...], (((1,), (1,)), ((), ())), preferred_element_type=F32
    )
    apart = jnp.sum(logits * (hits[0] - hits[1]), axis=-1, keepdims=True)
    shares_of = matches[0] * jax.nn.sigmoid(apart) + matches[1] * jax.nn.sigmoid(-apart)
    coarse = shares_of.astype(BF16)
    gates[c, 0] = coarse
    gates[c, 1] = (shares_of - coarse.astype(F32)).astype(BF16)
    pl.semaphore_wait(pltpu.get_barrier_semaphore(), len(friends))

    started = []

    def go(cp):
        cp.start()
        started.append(cp)
        return cp

    lasts = [
        go(remote(nsend, nbuf.at[c], e_s.at[0], e_r.at[0], sibling)),
        go(remote(pbuf.at[c], pbuf.at[c], e_s.at[1], e_r.at[1], sibling)),
        go(remote(gates.at[c], gates.at[c], e_s.at[2], e_r.at[2], sibling)),
    ]
    lasts[0].wait_recv()
    lasts[1].wait_recv()
    packed[...] = (
        lax.dot_general(
            pbuf[...].reshape(32, 128), nbuf[...].reshape(32, HALF), (((0,), (0,)), ((), ())),
            preferred_element_type=F32,
        )
        .astype(BF16)
        .reshape(E, TOK, HALF)
    )

    def part(i):
        return pl.ds(i * CW, CW)

    row = lax.broadcasted_iota(jnp.int32, (80, 128), 0)
    col = lax.broadcasted_iota(jnp.int32, (80, 128), 1)
    pick = (col == row // 10 * TOK + row % 10).astype(BF16)
    row = lax.broadcasted_iota(jnp.int32, (128, 80), 1)
    col = lax.broadcasted_iota(jnp.int32, (128, 80), 0)
    spread = (col == row // 10 * TOK + row % 10).astype(BF16)

    arrive = []
    for i in range(NCH):
        copies = []
        for d in range(1, 8):
            there = (req + d) % N_REQ
            copies.append(
                go(remote(
                    packed.at[there, :, part(i)], prx.at[i, req], a_s.at[i, d], a_r.at[i, d], peers[d - 1]
                ))
            )
        prx[i, req] = packed[req, :, i * CW : (i + 1) * CW]
        arrive.append(copies)

    def ring(n, i, src_at, dst_at, device):
        return go(remote(
            xo.at[(i,) + src_at], xo.at[(i,) + dst_at], g_s.at[n, i], g_r.at[n, i], device
        ))

    shares = {}

    def share(i, zr, y, second):
        at = zr * 2 + second
        shares[i, zr, second] = go(remote(
            xo.at[i, zr, y], xs.at[i, zr, y], f_s.at[at, i], f_r.at[at, i], sibling
        ))

    swap, up1, down1, up2, down2, up3, down3 = {}, {}, {}, {}, {}, {}, {}
    over1, over2, over3 = {}, {}, {}
    lower, upper = (slice(None), pl.ds(0, CUT)), (slice(None), pl.ds(CUT, CUT))
    for i in range(NCH):
        for cp in arrive[i]:
            cp.wait_recv()
        xo[i, 0, yh] = jnp.dot(
            pick, prx[i].reshape(128, CW), preferred_element_type=F32
        ).astype(BF16)
        swap[i] = ring(0, i, (0, yh), (0, yh), across)
        up1[i] = ring(1, i, (0, yh), (3, yh), up)
        down1[i] = ring(2, i, (0, yh), (1, yh), down)
        share(i, 0, yh, 0)
    for i in range(NCH):
        if i in LATE:
            up1[i].wait_recv()
            up3[i] = ring(5, i, (3, yh) + lower, (2, yh) + lower, up)
            over3[i] = ring(3, i, (3, yh), (3, yh), across)
            share(i, 3, yh, 0)
            down1[i].wait_recv()
            down3[i] = ring(6, i, (1, yh) + upper, (2, yh) + upper, down)
            over1[i] = ring(4, i, (1, yh), (1, yh), across)
            share(i, 1, yh, 0)
            swap[i].wait_recv()
            share(i, 0, other, 1)
        else:
            swap[i].wait_recv()
            up2[i] = ring(3, i, (0, other), (3, other), up)
            down2[i] = ring(4, i, (0, other), (1, other), down)
            share(i, 0, other, 1)
            up1[i].wait_recv()
            up3[i] = ring(5, i, (3, yh), (2, yh), up)
            share(i, 3, yh, 0)
            down1[i].wait_recv()
            share(i, 1, yh, 0)

    def hidden(i, zr):
        shares[i, zr, 0].wait_recv()
        shares[i, zr, 1].wait_recv()
        near = pl.ds(pl.multiple_of(c * HALF + i * CW, CW), CW)
        far = pl.ds(pl.multiple_of((1 - c) * HALF + i * CW, CW), CW)
        a, b = xo[i, zr].reshape(160, CW), xs[i, zr].reshape(160, CW)
        for n, weights in enumerate((wg, wu)):
            value = jnp.dot(a, weights[near, :], preferred_element_type=F32)
            value = value + jnp.dot(b, weights[far, :], preferred_element_type=F32)
            if i > 0:
                value = value + gu[zr, n]
            gu[zr, n] = value

    sums = {}

    def result(zr):
        inner[...] = (jax.nn.silu(gu[zr, 0]) * gu[zr, 1]).astype(BF16)
        for i in range(NCH):
            near = pl.ds(pl.multiple_of(c * HALF + i * CW, CW), CW)
            far = pl.ds(pl.multiple_of((1 - c) * HALF + i * CW, CW), CW)
            sps[i, zr] = (
                jnp.dot(inner[...], wd[:, far], preferred_element_type=F32)
                .astype(BF16)
                .reshape(2, 80, CW)
            )
            sums[i, zr] = go(remote(
                sps.at[i, zr], spr.at[i, zr], p_s.at[i, zr], p_r.at[i, zr], sibling
            ))
            po[i, zr] = (
                jnp.dot(inner[...], wd[:, near], preferred_element_type=F32)
                .astype(BF16)
                .reshape(2, 80, CW)
            )

    def total(i, zr, y):
        return po[i, zr, y].astype(F32) + spr[i, zr, y].astype(F32)

    def pass_on(n, i, value, device):
        rzs[n, i] = value.astype(BF16)
        return go(remote(rzs.at[n, i], rz.at[n, i], r_s.at[n, i], r_r.at[n, i], device))

    loads[0].wait()
    loads[1].wait()
    for i in range(NCH):
        hidden(i, 0)
    for i in range(NCH):
        if i in LATE:
            up3[i].wait_recv()
            down3[i].wait_recv()
            over2[i] = ring(7, i, (2, yh), (2, yh), across)
            share(i, 2, yh, 0)
            over1[i].wait_recv()
            share(i, 1, other, 1)
            over3[i].wait_recv()
            share(i, 3, other, 1)
        else:
            down2[i].wait_recv()
            down3[i] = ring(6, i, (1, other), (2, other), down)
            share(i, 1, other, 1)
            up2[i].wait_recv()
            share(i, 3, other, 1)
        hidden(i, 1)
        hidden(i, 3)
    loads[2].wait()
    result(1)
    result(3)
    early = [i for i in range(NCH) if i not in LATE]
    to_up, to_down, far_up, far_down, near_up, near_down = {}, {}, {}, {}, {}, {}
    cross, cross1, cross2, cross3, back = {}, {}, {}, {}, {}
    for i in range(NCH):
        sums[i, 1].wait_recv()
        sums[i, 3].wait_recv()
        if i in LATE:
            cross1[i] = pass_on(0, i, total(i, 1, other), across)
            cross3[i] = pass_on(1, i, total(i, 3, other), across)
        else:
            to_up[i] = pass_on(0, i, total(i, 1, other), up)
            to_down[i] = pass_on(1, i, total(i, 3, yh), down)
    for i in range(NCH):
        if i in LATE:
            over2[i].wait_recv()
            share(i, 2, other, 1)
        else:
            up3[i].wait_recv()
            share(i, 2, yh, 0)
            down3[i].wait_recv()
            share(i, 2, other, 1)
        if i > 0:
            hidden(i - 1, 2)
    hidden(NCH - 1, 2)
    result(2)
    for i in range(NCH):
        sums[i, 2].wait_recv()
        if i in LATE:
            cross2[i] = pass_on(6, i, total(i, 2, other), across)
        else:
            far_up[i] = pass_on(2, i, total(i, 2, yh), up)
            far_down[i] = pass_on(3, i, total(i, 2, other), down)
    result(0)

    def cross_over(i, value):
        ysend[i] = value.astype(BF16)
        cross[i] = go(remote(ysend.at[i], ry.at[i], y_s.at[i], y_r.at[i], across))

    for i in LATE:
        sums[i, 0].wait_recv()
        cross_over(i, total(i, 0, other))
        cross2[i].wait_recv()
        both = (total(i, 2, yh) + rz[6, i].astype(F32)).astype(BF16)
        rzs[2, i, :, :CUT] = both[:, :CUT]
        rzs[3, i, :, CUT:] = both[:, CUT:]
        for n, cols, device, copies in ((2, lower, up, far_up), (3, upper, down, far_down)):
            copies[i] = go(remote(
                rzs.at[(n, i) + cols], rz.at[(n, i) + cols], r_s.at[n, i], r_r.at[n, i], device
            ))
    for i in early:
        far_up[i].wait_recv()
        near_up[i] = pass_on(4, i, total(i, 1, yh) + rz[2, i].astype(F32), up)
        far_down[i].wait_recv()
        near_down[i] = pass_on(5, i, total(i, 3, other) + rz[3, i].astype(F32), down)
    for i in LATE:
        cross1[i].wait_recv()
        cross3[i].wait_recv()
        far_up[i].wait_recv()
        far_down[i].wait_recv()
        ahead = total(i, 1, yh) + rz[0, i].astype(F32)
        behind = total(i, 3, yh) + rz[1, i].astype(F32)
        added = jnp.concatenate(
            [ahead[:, :CUT] + rz[2, i, :, :CUT].astype(F32), ahead[:, CUT:]], axis=1
        )
        near_up[i] = pass_on(4, i, added, up)
        added = jnp.concatenate(
            [behind[:, :CUT], behind[:, CUT:] + rz[3, i, :, CUT:].astype(F32)], axis=1
        )
        near_down[i] = pass_on(5, i, added, down)

    def gathered(i):
        sums[i, 0].wait_recv()
        to_up[i].wait_recv()
        near_down[i].wait_recv()
        cross_over(i, total(i, 0, other) + rz[0, i].astype(F32) + rz[5, i].astype(F32))
        to_down[i].wait_recv()
        near_up[i].wait_recv()
        kept[i] = total(i, 0, yh) + rz[1, i].astype(F32) + rz[4, i].astype(F32)

    def give_back(i):
        cross[i].wait_recv()
        done = kept[i] + ry[i].astype(F32)
        if i in LATE:
            near_up[i].wait_recv()
            near_down[i].wait_recv()
            done = done + rz[4, i].astype(F32) + rz[5, i].astype(F32)
        bsend[i] = (
            jnp.dot(spread, done.astype(BF16), preferred_element_type=F32)
            .astype(BF16)
            .reshape(N_REQ, TOK, CW)
        )
        copies = []
        for d in range(1, 8):
            there = (req + d) % N_REQ
            copies.append(go(remote(
                bsend.at[i, there], ret.at[i, req], t_s.at[i, d], t_r.at[i, d], peers[d - 1]
            )))
        ret[i, req] = bsend[i, req]
        back[i] = copies

    for i in LATE:
        kept[i] = total(i, 0, yh)
    gathered(early[0])
    for n in range(1, len(early)):
        gathered(early[n])
        give_back(early[n - 1])
    give_back(early[-1])
    for i in LATE:
        give_back(i)
    mix = {}
    lasts[2].wait_recv()
    for i in early + list(LATE):
        for cp in back[i]:
            cp.wait_recv()
        terms = jnp.dot(
            gates[...].reshape(4 * TOK, 128), ret[i].reshape(128, CW), preferred_element_type=F32
        ).reshape(2, 2, TOK, CW)
        mixed[i] = terms[:, 0] + terms[:, 1]
        mix[i] = go(remote(mixed.at[i, 1 - c], mrecv.at[i], m_s.at[i], m_r.at[i], sibling))
        near = pl.ds(pl.multiple_of(c * HALF + i * CW, CW), CW)
        out[:, near] = (resid[:, near] + mixed[i, c]).astype(BF16)
    for i in early + list(LATE):
        mix[i].wait_recv()
        far = pl.ds(pl.multiple_of((1 - c) * HALF + i * CW, CW), CW)
        out[:, far] = (resid[:, far] + mrecv[i]).astype(BF16)
    for cp in started:
        cp.wait_send()


def experts(*operands):
    dma = pltpu.SemaphoreType.DMA
    v = pltpu.VMEM
    return pl.pallas_call(
        expert_kernel,
        out_shape=jax.ShapeDtypeStruct((TOK, D), BF16),
        in_specs=[VMEM] * 2 + [ANY] * 6,
        out_specs=VMEM,
        scratch_shapes=[
            v((TOK, D), BF16), v((1, D), F32), v((E, D), BF16), v((TOK, D), F32),
            v((E, TOK, HALF), BF16), v((TOK, HALF), BF16), v((2, TOK, HALF), BF16),
            v((2, TOK, 128), BF16), v((2, 2, TOK, 128), BF16),
            v((D, HID), BF16), v((D, HID), BF16), v((HID, D), BF16),
            v((NCH, N_REQ, TOK, CW), BF16),
            v((NCH, 4, 2, 80, CW), BF16), v((NCH, 4, 2, 80, CW), BF16),
            v((4, 2, 160, HID), F32),
            v((160, HID), BF16),
            v((NCH, 4, 2, 80, CW), BF16), v((NCH, 4, 2, 80, CW), BF16), v((NCH, 4, 2, 80, CW), BF16),
            v((7, NCH, 80, CW), BF16), v((7, NCH, 80, CW), BF16),
            v((NCH, 80, CW), BF16), v((NCH, 80, CW), BF16), v((NCH, 80, CW), F32),
            v((NCH, N_REQ, TOK, CW), BF16), v((NCH, N_REQ, TOK, CW), BF16),
            v((NCH, 2, TOK, CW), F32), v((NCH, TOK, CW), F32),
            dma((6,)), dma((3,)), dma((3,)), dma((NCH, 8)), dma((NCH, 8)), dma((NCH,)), dma((NCH,)),
            dma((8, NCH)), dma((8, NCH)), dma((8, NCH)), dma((8, NCH)),
            dma((NCH, 4)), dma((NCH, 4)), dma((7, NCH)), dma((7, NCH)),
            dma((NCH, 8)), dma((NCH, 8)), dma((NCH,)), dma((NCH,)),
        ],
        name="apply_experts",
        compiler_params=pltpu.CompilerParams(
            collective_id=1, has_side_effects=True, vmem_limit_bytes=60 << 20
        ),
    )(*operands)


def rotation(positions):
    steps = np.arange(HD // 2, dtype=np.float32) / np.float32(HD // 2)
    freq = (np.float64(ROPE_BASE) ** -steps.astype(np.float64)).astype(np.float32)
    angles = positions.astype(np.float32)[:, None] * freq[None, :]
    cosine, sine = np.cos(angles.astype(np.float64)), np.sin(angles.astype(np.float64))
    return (
        jnp.asarray(np.concatenate([cosine, cosine], axis=1), F32),
        jnp.asarray(np.concatenate([-sine, sine], axis=1), F32),
    )


def per_device(
    hidden_in, queries, question_kv, passage_kv, use_lists, offsets, out_weight, norm_gain,
    router, routes, w_gate, w_up, w_down,
):
    qcos, qsin = rotation(PUSE * (PLEN + GAP) + np.arange(QTOK))
    starts = np.arange(PUSE)[:, None] * (PLEN + GAP) + np.arange(GAP)[None, :]
    pcos, psin = rotation(starts.reshape(-1))
    attn = attention(
        jnp.concatenate([use_lists.T, offsets.T], axis=0), passage_kv, queries, question_kv,
        qcos, qsin, pcos, psin, out_weight,
    )
    return experts(
        attn, routes.T, hidden_in, norm_gain.reshape(1, D), router.T, w_gate[0], w_up[0], w_down[0]
    )


def solution(mesh):
    in_specs = (
        P(("req", "exp"), None),
        P("req", "exp"),
        P("req", None),
        P("req", "exp", None),
        P(),
        P(),
        P("exp", "req"),
        P(),
        P(),
        P(("req", "exp"), None),
        P("req", None, "exp"),
        P("req", None, "exp"),
        P("req", "exp", None),
    )
    return jax.shard_map(
        per_device, mesh=mesh, in_specs=in_specs, out_specs=P(("req", "exp"), None), check_vma=False
    )
```
